256 devices in a mesh: dp: 32 (over x, z_hi, y), tensor: 8 (over z_lo, core).
Axes of the slice: x: 4, y: 4, z: 8 (z_hi: 2, z_lo: 4; z = z_hi * 4 + z_lo), core: 2. Of those that a mesh axis runs over, the one named last changes fastest.
Arguments:
- context: bfloat16 [8192, 3072], P('dp', 'tensor'), may hold values from -6 to 6
- residual: bfloat16 [8192, 6144], P(('dp', 'tensor')), may hold values from -6 to 6
- out_proj: bfloat16 [6144, 3072], P('dp', 'tensor'), may hold values from -0.109375 to 0.109375
- norm_gain: float32 [6144], replicated, may hold values from 0.25 to 1.75
- cotangent: bfloat16 [8192, 6144], P(('dp', 'tensor')), may hold values from -0.75 to 0.75
- probe_seed: int32 [2], replicated, may hold values from 0 to 999999999
Outputs:
- hess_diag: float32 [6144, 3072], P('dp', 'tensor')
The draws below stay inside these ranges and needn't reach their ends.
All inputs are finite; a program needn't handle non-finite values.
Results may differ from the reference program's by a relative error of at most 0.0029.
Values may be sent and summed in bfloat16 or wider, within the bound.
No kernel may reach another device: no remote copies, remote signals or barrier semaphores. Data moves between devices by JAX's collectives and lax.ppermute only.
A program may use at most 128 MiB of HBM per device.

```python
import jax
import jax.numpy as jnp
from jax import lax

D = 6144
TOK = 256
HF = 3072
TOKENS = 8192


def strengthened(result, rng, source, target, blocks, factor):
    def block_of(dim):
        return (jnp.arange(result.shape[dim]) // (result.shape[dim] // blocks)).reshape((-1,) + (1,) * (result.ndim - 1 - dim))

    near = jax.random.permutation(rng, blocks)[block_of(target)]
    other_side = (block_of(target) + blocks // 2) % blocks
    return jnp.where((block_of(source) == near) | (block_of(source) == other_side), factor * result, result)


def level_of(rng, dims, split, least, top_value):
    gain, own = 1.0, jax.random.fold_in(rng, 6)
    for dim, blocks in split:
        steps = jnp.exp(jax.random.uniform(jax.random.fold_in(own, dim), (blocks,), jnp.float32, least / len(split), top_value / len(split)))
        gain = gain * jnp.repeat(steps, dims[dim] // blocks).reshape([-1 if axis == dim else 1 for axis in range(len(dims))])
    return gain


def gaussian(stream_key, extent, spread, bound, pieces=(), kind=jnp.bfloat16):
    array = spread * jax.random.normal(stream_key, extent, jnp.float32)
    if pieces:
        array = array * level_of(stream_key, extent, pieces, -0.22, 0.18)
    return jnp.clip(array, -bound, bound).astype(kind)


def bell_draw_with(own_key, shape, width, limit, shards, heavy, dtype=jnp.bfloat16):
    drawn = width * jax.random.normal(own_key, shape, jnp.float32)
    if shards:
        drawn = drawn * level_of(own_key, shape, shards, -0.22, 0.18)
    return jnp.clip(strengthened(drawn, jax.random.fold_in(own_key, 3), *heavy), -limit, limit).astype(dtype)


def setup_inputs(seed: int = 0) -> dict:
    seeds = jax.random.split(jax.random.key(seed), 7)
    return {
        "context": gaussian(seeds[0], (TOKENS, HF), 1.0, 6.0, ((0, 32), (1, 8))),
        "residual": gaussian(seeds[1], (TOKENS, D), 1.0, 6.0, ((0, 256),)),
        "out_proj": gaussian(seeds[2], (D, HF), HF ** -0.5, 0.109375, ((0, 32), (1, 8))),
        "norm_gain": jnp.clip(1.0 + 0.15 * jax.random.normal(seeds[3], (D,), jnp.float32), 0.25, 1.75),
        "cotangent": bell_draw_with(seeds[4], (TOKENS, D), (8.0 / TOK), 0.75, ((0, 256),), (0, 1, 256, 6.0)),
        "probe_seed": jax.random.randint(seeds[5], (2,), 0, 1000000000).astype(jnp.int32),
    }


def probe_signs(seed_pair, row_ids, col_ids, full_width):
    flat_index = row_ids[:, None].astype(jnp.int32) * jnp.int32(full_width) + col_ids[None, :].astype(jnp.int32)
    mixed = flat_index * jnp.int32(747796405) + seed_pair[0]
    mixed = mixed ^ lax.shift_right_logical(mixed, jnp.int32(16))
    mixed = mixed * jnp.int32(73244475)
    mixed = mixed ^ seed_pair[1]
    mixed = mixed ^ lax.shift_right_logical(mixed, jnp.int32(15))
    parity = lax.shift_right_logical(mixed, jnp.int32(9)) & jnp.int32(1)
    return (jnp.int32(1) - jnp.int32(2) * parity).astype(jnp.bfloat16)

def norm_gradient(stream, norm_gain, cotangent):

    def linear_loss(values):
        row_mean = lax.optimization_barrier(jnp.mean(values, axis=-1, keepdims=True))
        centered = values - row_mean
        variance = lax.optimization_barrier(jnp.mean(centered * centered, axis=-1, keepdims=True))
        normed = centered * lax.rsqrt(variance + 1e-05)
        return jnp.sum(cotangent.astype(jnp.float32) * norm_gain.astype(jnp.float32) * normed)
    return jax.grad(linear_loss)(stream)

def reference(context, residual, out_proj, norm_gain, cotangent, probe_seed):
    model_width = out_proj.shape[0]
    feature_count = out_proj.shape[1]
    probe = probe_signs(probe_seed, jnp.arange(model_width).astype(jnp.int32), jnp.arange(feature_count).astype(jnp.int32), feature_count)
    primal = jnp.dot(context, out_proj.T, preferred_element_type=jnp.float32)
    tangent = jnp.dot(context, probe.T, preferred_element_type=jnp.float32)
    stream = residual.astype(jnp.float32) + primal
    tangent_grad = jax.jvp(lambda values: norm_gradient(values, norm_gain, cotangent), (stream,), (tangent,))[1]
    tangent_grad = tangent_grad.astype(jnp.bfloat16)
    curvature = lax.dot_general(tangent_grad, context, (((0,), (0,)), ((), ())), preferred_element_type=jnp.float32)
    return probe.astype(jnp.float32) * curvature
```

```python
import jax
import jax.numpy as jnp
from jax import lax
from jax.experimental import pallas as pl
from jax.experimental.pallas import tpu as pltpu
from jax.sharding import Mesh
from jax.sharding import PartitionSpec as P

AXES = ("x", "zh", "y", "zl", "c")
GRID = (4, 2, 4, 4, 2)
Z = ("zh", "zl")
XY = ("x", "y")
T = ("zl", "c")
R = 192
F = 384
W = 8 * F
OWN = 32
HALF = OWN // 2
TOK = 16 * OWN
D = 2 * R
N = 32 * R
VMEM = 48 * 1024 * 1024
MULT = 747796405
INT = jnp.int32
F32 = jnp.float32
BF16 = jnp.bfloat16
NT = (((1,), (1,)), ((), ()))


def shift(v, axis, k):
    n = 8 if axis == Z else 4
    return lax.ppermute(v, axis, [(s, (s + k) % n) for s in range(n)])


def probe_kernel(info, out):
    x, y, seed0, seed1 = info[0], info[1], info[4], info[5]
    cols = lax.broadcasted_iota(INT, (1, F), 1) + pl.program_id(0) * F
    rows = lax.broadcasted_iota(INT, (R, 1), 0)
    for zh in range(2):
        d = rows + (x * 8 + zh * 4 + y) * R
        m = (d * W * INT(MULT) + seed0) + cols * INT(MULT)
        m = m ^ lax.shift_right_logical(m, INT(16))
        m = m * INT(73244475)
        m = m ^ seed1
        m = m ^ lax.shift_right_logical(m, INT(15))
        parity = lax.shift_right_logical(m, INT(9)) & INT(1)
        out[zh * R : (zh + 1) * R, :] = (1 - 2 * parity).astype(F32).astype(BF16)


def make_probe(info):
    return pl.pallas_call(
        probe_kernel,
        grid=(8,),
        in_specs=[pl.BlockSpec(memory_space=pltpu.SMEM)],
        out_specs=pl.BlockSpec((D, F), lambda j: (0, j)),
        out_shape=jax.ShapeDtypeStruct((D, W), BF16),
        compiler_params=pltpu.CompilerParams(vmem_limit_bytes=VMEM),
        cost_estimate=pl.CostEstimate(flops=14 * D * W, bytes_accessed=2 * D * W, transcendentals=0),
    )(info)


def chip_of(i, zr):
    k = (i % 2) * 4 + i // 2
    return k, (zr - k + 8) % 8


def forward_kernel(info, *refs):
    pieces, (own, other, probe, rc, gain), (context, s_out, u_out, w_out, stats), (acc_p, acc_u) = (
        refs[:8],
        refs[8:13],
        refs[13:18],
        refs[18:],
    )
    i = pl.program_id(0)
    x, y, zr, c = info[0], info[1], info[2], info[3]
    zh = chip_of(i, zr)[1] // 4

    @pl.when(i == 0)
    def _():
        acc_p[...] = jnp.zeros_like(acc_p)
        acc_u[...] = jnp.zeros_like(acc_u)

    @pl.when(i % 2 == 0)
    def _():
        for first in range(4):
            for second in range(4):
                ax, ay = (x - second + 4) % 4, (y - first + 4) % 4
                row = pl.multiple_of((ax * 4 + ay) * OWN, OWN)
                context[pl.ds(row, HALF), :] = pieces[first][second]
                ax, ay = (x - first + 4) % 4, (y - second + 4) % 4
                row = pl.multiple_of((ax * 4 + ay) * OWN + HALF, HALF)
                context[pl.ds(row, HALF), :] = pieces[4 + first][second]

    mine = context[:, pl.ds(pl.multiple_of(c * F, F), F)]
    theirs = context[:, pl.ds(pl.multiple_of((1 - c) * F, F), F)]
    acc_p[zh] += lax.dot_general(own[0], mine, NT, preferred_element_type=F32) + lax.dot_general(
        other[0], theirs, NT, preferred_element_type=F32
    )
    acc_u[zh] += lax.dot_general(probe[...], context[...], NT, preferred_element_type=F32)

    @pl.when(i == 7)
    def _():
        eye = (lax.broadcasted_iota(INT, (D, D), 0) == lax.broadcasted_iota(INT, (D, D), 1)).astype(F32).astype(BF16)
        residual = rc[:, 0].reshape(TOK, D)
        cotangent = rc[:, 1].reshape(TOK, D)
        s = lax.dot_general(eye, residual, NT, preferred_element_type=F32) + acc_p[...].reshape(D, TOK)
        u = acc_u[...].reshape(D, TOK)
        w = lax.dot_general(eye, cotangent, NT, preferred_element_type=F32) * gain[...]
        s_out[...] = s
        u_out[...] = u
        w_out[...] = w
        mean = lambda v: jnp.sum(v, axis=0, keepdims=True) * (1.0 / D)
        ms, mu, mw = mean(s), mean(u), mean(w)
        sc, uc, wc = s - ms, u - mu, w - mw
        stats[0:1] = ms
        stats[1:2] = mu
        stats[2:3] = mw
        stats[3:4] = mean(sc * sc)
        stats[4:5] = mean(sc * uc)
        stats[5:6] = mean(sc * wc)
        stats[6:7] = mean(uc * wc)
        stats[7:8] = jnp.zeros_like(ms)


def forward(info, pieces, own, other, probe, rc, gain):
    whole = lambda *shape: pl.BlockSpec(shape, lambda i, info: (0,) * len(shape))
    zl = lambda i, info: chip_of(i, info[2])[1] % 4
    zh = lambda i, info: chip_of(i, info[2])[1] // 4
    return pl.pallas_call(
        forward_kernel,
        grid_spec=pltpu.PrefetchScalarGridSpec(
            num_scalar_prefetch=1,
            grid=(8,),
            in_specs=[pl.BlockSpec((4, HALF, 2 * F), lambda i, info: (0, 0, zl(i, info)))] * 8
            + [pl.BlockSpec((1, R, F), lambda i, info: (chip_of(i, info[2])[0], 0, 0))] * 2
            + [
                pl.BlockSpec((R, 2 * F), lambda i, info: (zh(i, info), zl(i, info))),
                whole(16, 2, OWN, D),
                whole(D, 1),
            ],
            out_specs=[pl.BlockSpec((TOK, 2 * F), lambda i, info: (0, zl(i, info)))]
            + [whole(D, TOK)] * 3
            + [whole(8, TOK)],
            scratch_shapes=[pltpu.VMEM((2, R, TOK), F32)] * 2,
        ),
        out_shape=[jax.ShapeDtypeStruct((TOK, W), BF16)]
        + [jax.ShapeDtypeStruct((D, TOK), F32)] * 3
        + [jax.ShapeDtypeStruct((8, TOK), F32)],
        compiler_params=pltpu.CompilerParams(vmem_limit_bytes=VMEM),
        cost_estimate=pl.CostEstimate(flops=4 * D * TOK * W, bytes_accessed=12 * TOK * W, transcendentals=0),
    )(info, *pieces, own, other, probe, rc, gain)


def curvature_kernel(info, stats, s, u, w, context, send, keep, grad):
    c = info[3]

    @pl.when(pl.program_id(0) == 0)
    def _():
        parts = [stats[j] for j in range(16)]
        total = parts[0]
        for part in parts[1:]:
            total = total + part
        mean = total * (1.0 / 16)
        ms, mu, mw = mean[0:1], mean[1:2], mean[2:3]
        css, csu, csw, cuw = mean[3:4], mean[4:5], mean[5:6], mean[6:7]
        for part in parts:
            ds, du, dw = part[0:1] - ms, part[1:2] - mu, part[2:3] - mw
            css = css + ds * ds * (1.0 / 16)
            csu = csu + ds * du * (1.0 / 16)
            csw = csw + ds * dw * (1.0 / 16)
            cuw = cuw + du * dw * (1.0 / 16)
        r2 = 1.0 / (css + 1e-05)
        r = lax.rsqrt(css + 1e-05)
        k = -(r * r2)
        gamma = cuw - 3.0 * r2 * csu * csw
        value = k * (csu * (w[...] - mw) + csw * (u[...] - mu) + gamma * (s[...] - ms))
        grad[...] = value.astype(BF16)

    mine = context[:, pl.ds(pl.multiple_of(c * F, F), F)]
    theirs = context[:, pl.ds(pl.multiple_of((1 - c) * F, F), F)]
    send[:, 0] = jnp.dot(grad[...], theirs, preferred_element_type=F32).astype(BF16).reshape(2, R, F)
    keep[:, 0] = jnp.dot(grad[...], mine, preferred_element_type=F32).reshape(2, R, F)


def curvature_parts(info, stats, s, u, w, context):
    whole = lambda *shape: pl.BlockSpec(shape, lambda i, info: (0,) * len(shape))
    out = pl.BlockSpec((2, 1, R, F), lambda i, info: (0, i, 0, 0))
    return pl.pallas_call(
        curvature_kernel,
        grid_spec=pltpu.PrefetchScalarGridSpec(
            num_scalar_prefetch=1,
            grid=(4,),
            in_specs=[whole(16, 8, TOK)]
            + [whole(D, TOK)] * 3
            + [pl.BlockSpec((TOK, 2 * F), lambda i, info: (0, i))],
            out_specs=[out, out],
            scratch_shapes=[pltpu.VMEM((D, TOK), BF16)],
        ),
        out_shape=[
            jax.ShapeDtypeStruct((2, 4, R, F), BF16),
            jax.ShapeDtypeStruct((2, 4, R, F), F32),
        ],
        compiler_params=pltpu.CompilerParams(vmem_limit_bytes=VMEM),
        cost_estimate=pl.CostEstimate(flops=2 * D * TOK * W, bytes_accessed=8 * TOK * W, transcendentals=0),
    )(info, stats, s, u, w, context)


def ring_blocks(block):
    behind, ahead = [block], [block]
    for _ in range(3):
        behind.append(shift(behind[-1], Z, 1))
        ahead.append(shift(ahead[-1], Z, -1))
    h = R // 2
    far = jnp.concatenate([shift(behind[-1][:h], Z, 1), shift(ahead[-1][h:], Z, -1)], 0)
    return jnp.stack(behind + [far] + ahead[:0:-1])


def plane_blocks(blocks, axes):
    near = [(shift(v, a, 1), shift(v, a, -1)) for v, a in zip(blocks, axes)]
    out = []
    for (behind, ahead), v, a in zip(near, blocks, axes):
        h = v.shape[0] // 2
        far = jnp.concatenate([shift(behind[:h], a, 1), shift(ahead[h:], a, -1)], 0)
        out.append((v, behind, far, ahead))
    return out


def on_device(context, residual, out_proj, norm_gain, cotangent, probe_seed):
    x, zh, y, zl, c = (lax.axis_index(a).astype(INT) for a in AXES)
    info = jnp.concatenate([jnp.stack([x, y, zh * 4 + zl, c]), probe_seed])

    probe = make_probe(info)
    own = ring_blocks(out_proj)
    other = lax.ppermute(own, "c", [(0, 1), (1, 0)])

    rows = lax.all_to_all(context, T, 0, 1, tiled=True)
    a, b = plane_blocks([rows[:HALF], rows[HALF:]], ["x", "y"])
    a, b = plane_blocks([jnp.stack(a), jnp.stack(b)], ["y", "x"])

    rc = jnp.stack([residual, cotangent]).reshape(2, OWN, 4, 2, 4, R)
    rc = rc.transpose(2, 4, 0, 1, 3, 5).reshape(16, 2, OWN, D)
    rc = lax.all_to_all(rc, XY, 0, 0, tiled=True)
    gain = norm_gain.reshape(4, 2, 4, R)
    gain = lax.dynamic_index_in_dim(lax.dynamic_index_in_dim(gain, x, 0, False), y, 1, False).reshape(D, 1)

    rows, s, u, w, stats = forward(info, [*a, *b], own, other, probe, rc, gain)
    stats = lax.all_to_all(jnp.broadcast_to(stats[None], (16, 8, TOK)), XY, 0, 0, tiled=True)
    send, keep = curvature_parts(info, stats, s, u, w, rows)
    total = (keep + lax.ppermute(send, "c", [(0, 1), (1, 0)]).astype(F32)).astype(BF16)
    total = lax.all_to_all(total.reshape(8, R, F), Z, 0, 0, tiled=True)
    curvature = jnp.sum(total.astype(F32), axis=0)
    signs = lax.dynamic_slice(probe, (zh * R, (zl * 2 + c) * F), (R, F))
    return signs.astype(F32) * curvature


def solution(mesh):
    split = Mesh(mesh.devices.reshape(GRID), AXES)
    dp, tensor = ("x", "zh", "y"), T
    in_specs = (
        P(dp, tensor),
        P((*dp, *tensor), None),
        P(dp, tensor),
        P(),
        P((*dp, *tensor), None),
        P(),
    )
    return jax.shard_map(on_device, mesh=split, in_specs=in_specs, out_specs=P(dp, tensor), check_vma=False)
```

```python
import jax
import jax.numpy as jnp
from jax import lax
from jax.experimental import pallas as pl
from jax.experimental.pallas import tpu as pltpu
from jax.sharding import Mesh
from jax.sharding import PartitionSpec as P

AXES = ("x", "zh", "y", "zl", "c")
GRID = (4, 2, 4, 4, 2)
Z = ("zh", "zl")
XY = ("x", "y")
T = ("zl", "c")
R = 192
F = 384
W = 8 * F
OWN = 32
TOK = 16 * OWN
D = 2 * R
N = 32 * R
E = W + 2 * D
XYC = ("x", "y", "c")
MIB = 1024 * 1024
MULT = 747796405
INT = jnp.int32
F32 = jnp.float32
BF16 = jnp.bfloat16
NT = (((1,), (1,)), ((), ()))


def shift(v, axis, k):
    n = 8 if axis == Z else 4
    return lax.ppermute(v, axis, [(s, (s + k) % n) for s in range(n)])


def probe_kernel(info, out):
    x, y, seed0, seed1 = info[0], info[1], info[4], info[5]
    cols = lax.broadcasted_iota(INT, (1, F), 1) + pl.program_id(0) * F
    rows = lax.broadcasted_iota(INT, (R, 1), 0)
    for zh in range(2):
        d = rows + (x * 8 + zh * 4 + y) * R
        m = (d * W * INT(MULT) + seed0) + cols * INT(MULT)
        m = m ^ lax.shift_right_logical(m, INT(16))
        m = m * INT(73244475)
        m = m ^ seed1
        m = m ^ lax.shift_right_logical(m, INT(15))
        parity = lax.shift_right_logical(m, INT(9)) & INT(1)
        out[zh * R : (zh + 1) * R, :] = (1 - 2 * parity).astype(F32).astype(BF16)


def make_probe(info):
    return pl.pallas_call(
        probe_kernel,
        grid=(8,),
        in_specs=[pl.BlockSpec(memory_space=pltpu.SMEM)],
        out_specs=pl.BlockSpec((D, F), lambda j: (0, j)),
        out_shape=jax.ShapeDtypeStruct((D, W), BF16),
        compiler_params=pltpu.CompilerParams(vmem_limit_bytes=16 * MIB),
        cost_estimate=pl.CostEstimate(flops=14 * D * W, bytes_accessed=2 * D * W, transcendentals=0),
    )(info)


def regroup_kernel(info, residual, cotangent, gains, out, gain):
    x, y, c = info[0], info[1], info[3]
    eye = lax.broadcasted_iota(INT, (R, R), 0) == lax.broadcasted_iota(INT, (R, R), 1)
    for zh in range(2):
        row = gains[pl.ds(x * 8 + zh * 4 + y, 1), :]
        gain[zh * R : (zh + 1) * R, :] = jnp.sum(jnp.where(eye, row, 0.0), axis=1, keepdims=True)

    @pl.when(c == 0)
    def _():
        for n, v in enumerate((residual, cotangent)):
            for k in range(4):
                part = v[:, pl.ds(pl.multiple_of((x + k) % 4 * (8 * R), 8 * R), 8 * R)]
                for at in range(4):
                    for zh in range(2):
                        first = at * 2 * D + n * D + zh * R
                        out[k, :, first : first + R] = part[:, (zh * 4 + at) * R : (zh * 4 + at + 1) * R]

    @pl.when(c == 1)
    def _():
        for n, v in enumerate((residual, cotangent)):
            for at in range(4):
                part = v[:, at * 8 * R : (at + 1) * 8 * R]
                for to in range(4):
                    k = (to - y + 4) % 4
                    for zh in range(2):
                        first = at * 2 * D + n * D + zh * R
                        out[k, :, first : first + R] = part[:, (zh * 4 + to) * R : (zh * 4 + to + 1) * R]


def regroup(info, residual, cotangent, norm_gain):
    return pl.pallas_call(
        regroup_kernel,
        in_specs=[pl.BlockSpec(memory_space=pltpu.SMEM)] + [pl.BlockSpec(memory_space=pltpu.VMEM)] * 3,
        out_shape=[jax.ShapeDtypeStruct((4, OWN, 8 * D), BF16), jax.ShapeDtypeStruct((D, 1), F32)],
        compiler_params=pltpu.CompilerParams(vmem_limit_bytes=16 * MIB),
        cost_estimate=pl.CostEstimate(flops=0, bytes_accessed=8 * OWN * N, transcendentals=0),
    )(info, residual, cotangent, norm_gain.reshape(32, R))


def first_kernel(rows, rest, *out):
    for k in range(4):
        for t in range(8):
            out[k][:OWN, t * F : (t + 1) * F] = rows[t]
        out[k][OWN:] = rest[k]


def first_leg(rows, rest):
    return pl.pallas_call(
        first_kernel,
        out_shape=[jax.ShapeDtypeStruct((2 * OWN, W), BF16)] * 4,
        compiler_params=pltpu.CompilerParams(vmem_limit_bytes=16 * MIB),
        cost_estimate=pl.CostEstimate(flops=0, bytes_accessed=32 * OWN * W, transcendentals=0),
    )(rows, rest)


def second_kernel(info, *refs):
    came, out = refs[:4], refs[4:]
    place = jnp.where(info[3] == 0, info[1], info[0])
    for j in range(4):
        columns = pl.ds(pl.multiple_of((place + j) % 4 * 2 * D, 2 * D), 2 * D)
        for k in range(4):
            out[j][k, :, :W] = came[k][:OWN]
            out[j][k, :, W:] = came[k][OWN:, columns]


def second_leg(info, came):
    return pl.pallas_call(
        second_kernel,
        in_specs=[pl.BlockSpec(memory_space=pltpu.SMEM)] + [pl.BlockSpec(memory_space=pltpu.VMEM)] * 4,
        out_shape=[jax.ShapeDtypeStruct((4, OWN, E), BF16)] * 4,
        compiler_params=pltpu.CompilerParams(vmem_limit_bytes=16 * MIB),
        cost_estimate=pl.CostEstimate(flops=0, bytes_accessed=64 * OWN * E, transcendentals=0),
    )(info, *came)


def tangent_kernel(info, *refs):
    pieces, (probe, gain), (context, residual, u_out, w_out), cotangent = refs[:4], refs[4:6], refs[6:10], refs[10]
    x, y, c = info[0], info[1], info[3]
    for j in range(4):
        for k in range(4):
            ax = (x - jnp.where(c == 0, k, j) + 4) % 4
            ay = (y - jnp.where(c == 0, j, k) + 4) % 4
            row = pl.ds(pl.multiple_of((ax * 4 + ay) * OWN, OWN), OWN)
            context[row, :] = pieces[j][k, :, :W]
            residual[row, :] = pieces[j][k, :, W : W + D]
            cotangent[row, :] = pieces[j][k, :, W + D :]
    u_out[...] = lax.dot_general(probe[...], context[...], NT, preferred_element_type=F32)
    w_out[...] = turned(cotangent[...]) * gain[...]


def turned(v):
    eye = (lax.broadcasted_iota(INT, (D, D), 0) == lax.broadcasted_iota(INT, (D, D), 1)).astype(F32).astype(BF16)
    return lax.dot_general(eye, v, NT, preferred_element_type=F32)


def tangent_of(info, pieces, probe, gain):
    return pl.pallas_call(
        tangent_kernel,
        in_specs=[pl.BlockSpec(memory_space=pltpu.SMEM)] + [pl.BlockSpec(memory_space=pltpu.VMEM)] * 6,
        out_shape=[jax.ShapeDtypeStruct((TOK, W), BF16), jax.ShapeDtypeStruct((TOK, D), BF16)]
        + [jax.ShapeDtypeStruct((D, TOK), F32)] * 2,
        scratch_shapes=[pltpu.VMEM((TOK, D), BF16)],
        compiler_params=pltpu.CompilerParams(vmem_limit_bytes=16 * MIB),
        cost_estimate=pl.CostEstimate(flops=2 * D * TOK * W, bytes_accessed=8 * TOK * W, transcendentals=0),
    )(info, *pieces, probe, gain)


def stream_kernel(info, own, other, context, residual, u_in, w_in, s_out, stats, weight):
    zr, c = info[2], info[3]
    for zh in range(2):
        for zl in range(4):
            at = (zr - (zh * 4 + zl) + 8) % 8
            rows = slice(zh * R, (zh + 1) * R)
            weight[rows, pl.ds(pl.multiple_of((zl * 2 + c) * F, F), F)] = own[at]
            weight[rows, pl.ds(pl.multiple_of((zl * 2 + 1 - c) * F, F), F)] = other[at]
    s = turned(residual[...]) + lax.dot_general(weight[...], context[...], NT, preferred_element_type=F32)
    s_out[...] = s
    u, w = u_in[...], w_in[...]
    mean = lambda v: jnp.sum(v, axis=0, keepdims=True) * (1.0 / D)
    ms, mu, mw = mean(s), mean(u), mean(w)
    sc, uc, wc = s - ms, u - mu, w - mw
    stats[0:1] = ms
    stats[1:2] = mu
    stats[2:3] = mw
    stats[3:4] = mean(sc * sc)
    stats[4:5] = mean(sc * uc)
    stats[5:6] = mean(sc * wc)
    stats[6:7] = mean(uc * wc)
    stats[7:8] = jnp.zeros_like(ms)


def stream_of(info, own, other, context, residual, u, w):
    return pl.pallas_call(
        stream_kernel,
        in_specs=[pl.BlockSpec(memory_space=pltpu.SMEM)] + [pl.BlockSpec(memory_space=pltpu.VMEM)] * 6,
        out_shape=[jax.ShapeDtypeStruct((D, TOK), F32), jax.ShapeDtypeStruct((8, TOK), F32)],
        scratch_shapes=[pltpu.VMEM((D, W), BF16)],
        compiler_params=pltpu.CompilerParams(vmem_limit_bytes=16 * MIB),
        cost_estimate=pl.CostEstimate(flops=2 * D * TOK * W, bytes_accessed=8 * TOK * W, transcendentals=0),
    )(info, own, other, context, residual, u, w)


def gradient(stats, s, u, w):
    parts = [stats[j] for j in range(16)]
    total = parts[0]
    for part in parts[1:]:
        total = total + part
    mean = total * (1.0 / 16)
    ms, mu, mw = mean[0:1], mean[1:2], mean[2:3]
    css, csu, csw, cuw = mean[3:4], mean[4:5], mean[5:6], mean[6:7]
    for part in parts:
        ds, du, dw = part[0:1] - ms, part[1:2] - mu, part[2:3] - mw
        css = css + ds * ds * (1.0 / 16)
        csu = csu + ds * du * (1.0 / 16)
        csw = csw + ds * dw * (1.0 / 16)
        cuw = cuw + du * dw * (1.0 / 16)
    r2 = 1.0 / (css + 1e-05)
    r = lax.rsqrt(css + 1e-05)
    k = -(r * r2)
    gamma = cuw - 3.0 * r2 * csu * csw
    value = k * (csu * (w[...] - mw) + csw * (u[...] - mu) + gamma * (s[...] - ms))
    return value.astype(BF16)


def owner(info, k):
    chip = (info[2] + k) % 8
    return pl.ds(pl.multiple_of(chip // 4 * R, R), R), chip % 4 * 2


def away_kernel(info, stats, s, u, w, context, grad, send):
    grad[...] = gradient(stats, s, u, w)
    for k in range(8):
        rows, feature = owner(info, k)
        columns = context[:, pl.ds(pl.multiple_of((feature + 1 - info[3]) * F, F), F)]
        send[k] = jnp.dot(grad[rows, :], columns, preferred_element_type=F32).astype(BF16)


def away(info, stats, s, u, w, context):
    return pl.pallas_call(
        away_kernel,
        in_specs=[pl.BlockSpec(memory_space=pltpu.SMEM)] + [pl.BlockSpec(memory_space=pltpu.VMEM)] * 5,
        out_shape=[jax.ShapeDtypeStruct((D, TOK), BF16), jax.ShapeDtypeStruct((8, R, F), BF16)],
        compiler_params=pltpu.CompilerParams(vmem_limit_bytes=16 * MIB),
        cost_estimate=pl.CostEstimate(flops=D * TOK * W, bytes_accessed=8 * TOK * W, transcendentals=0),
    )(info, stats, s, u, w, context)


def home_kernel(info, grad, context, received, near_up, near_down, three_up, three_down, four_up, four_down, kept):
    def part(k):
        rows, feature = owner(info, k)
        columns = context[:, pl.ds(pl.multiple_of((feature + info[3]) * F, F), F)]
        return jnp.dot(grad[rows, :], columns, preferred_element_type=F32) + received[k].astype(F32)

    three_up[...] = part(3).astype(BF16)
    three_down[...] = part(5).astype(BF16)
    four = part(4).astype(BF16)
    four_up[...] = four[: R // 2]
    four_down[...] = four[R // 2 :]
    near_up[...] = part(1).astype(BF16)
    near_down[...] = part(7).astype(BF16)
    for n, k in enumerate((0, 2, 6)):
        kept[n] = part(k)


def home(info, grad, context, received):
    return pl.pallas_call(
        home_kernel,
        in_specs=[pl.BlockSpec(memory_space=pltpu.SMEM)] + [pl.BlockSpec(memory_space=pltpu.VMEM)] * 3,
        out_shape=[jax.ShapeDtypeStruct((R, F), BF16)] * 4
        + [jax.ShapeDtypeStruct((R // 2, F), BF16)] * 2
        + [jax.ShapeDtypeStruct((3, R, F), F32)],
        compiler_params=pltpu.CompilerParams(vmem_limit_bytes=16 * MIB),
        cost_estimate=pl.CostEstimate(flops=D * TOK * W, bytes_accessed=8 * TOK * W, transcendentals=0),
    )(info, grad, context, received)


def swap(v):
    return lax.ppermute(v, "c", [(0, 1), (1, 0)])


def after(v, *others):
    return lax.optimization_barrier((v, *others))[0]


def leg(blocks, axes):
    out = [blocks[0]]
    for k in range(1, 4):
        pairs = []
        for x in range(4):
            for y in range(4):
                for c in range(2):
                    to = ((x + k) % 4, y) if axes[c] == "x" else (x, (y + k) % 4)
                    pairs.append(((x * 4 + y) * 2 + c, (to[0] * 4 + to[1]) * 2 + c))
        out.append(lax.ppermute(blocks[k], XYC, pairs))
    return out


def on_device(context, residual, out_proj, norm_gain, cotangent, probe_seed):
    x, zh, y, zl, c = (lax.axis_index(a).astype(INT) for a in AXES)
    info = jnp.concatenate([jnp.stack([x, y, zh * 4 + zl, c]), probe_seed])

    rest, gain = regroup(info, residual, cotangent, norm_gain)
    rows = lax.all_to_all(context.reshape(8, OWN, F), T, 0, 0, tiled=True)
    rows, rest, gain = lax.optimization_barrier((rows, rest, gain))

    came = lax.optimization_barrier(leg(first_leg(rows, rest), "xy"))
    behind, ahead = shift(out_proj, Z, 1), shift(out_proj, Z, -1)
    two, ahead2 = after(jnp.stack([out_proj, behind]), rows), after(jnp.stack([out_proj, ahead]), rows)
    behind2, ahead2 = shift(two, Z, 2), shift(ahead2, Z, -2)
    far = shift(after(ahead2[1], *came), Z, -1)
    own = jnp.concatenate([two, behind2, far[None], ahead2[::-1], ahead[None]])

    probe = make_probe(after(info, *came))
    *pieces, probe, own = lax.optimization_barrier((*leg(second_leg(info, came), "yx"), probe, own))
    other = swap(own)
    rows, res, u, w = tangent_of(info, pieces, probe, gain)
    s, stats = stream_of(info, own, other, rows, res, u, w)
    stats = lax.all_to_all(jnp.broadcast_to(stats[None], (16, 8, TOK)), XY, 0, 0, tiled=True)
    grad, send = away(info, stats, s, u, w, rows)
    near_up, near_down, three_up, three_down, four_up, four_down, kept = home(info, grad, rows, swap(send))

    near_up, near_down, three_up, three_down, four_up, four_down = lax.optimization_barrier(
        (
            shift(near_up, Z, 1),
            shift(near_down, Z, -1),
            shift(three_up, Z, 1),
            shift(three_down, Z, -1),
            shift(four_up, Z, 2),
            shift(four_down, Z, -2),
        )
    )
    none = jnp.zeros((R // 2, F), F32)
    up = kept[1] + three_up.astype(F32) + jnp.concatenate([four_up.astype(F32), none])
    down = kept[2] + three_down.astype(F32) + jnp.concatenate([none, four_down.astype(F32)])
    up, down = shift(up.astype(BF16), Z, 2), shift(down.astype(BF16), Z, -2)
    total = kept[0] + near_up.astype(F32) + near_down.astype(F32) + up.astype(F32) + down.astype(F32)
    signs = lax.dynamic_slice(probe, (zh * R, (zl * 2 + c) * F), (R, F))
    return signs.astype(F32) * total


def solution(mesh):
    split = Mesh(mesh.devices.reshape(GRID), AXES)
    dp, tensor = ("x", "zh", "y"), T
    in_specs = (
        P(dp, tensor),
        P((*dp, *tensor), None),
        P(dp, tensor),
        P(),
        P((*dp, *tensor), None),
        P(),
    )
    return jax.shard_map(on_device, mesh=split, in_specs=in_specs, out_specs=P(dp, tensor), check_vma=False)
```

```python
import jax
import jax.numpy as jnp
from jax import lax
from jax.experimental import pallas as pl
from jax.experimental.pallas import tpu as pltpu
from jax.sharding import Mesh
from jax.sharding import PartitionSpec as P

AXES = ("x", "zh", "y", "zl", "c")
GRID = (4, 2, 4, 4, 2)
Z = ("zh", "zl")
XY = ("x", "y")
T = ("zl", "c")
R = 192
F = 384
W = 8 * F
OWN = 32
TOK = 16 * OWN
D = 2 * R
N = 32 * R
E = W + 2 * D
XYC = ("x", "y", "c")
MIB = 1024 * 1024
MULT = 747796405
INT = jnp.int32
F32 = jnp.float32
BF16 = jnp.bfloat16
NT = (((1,), (1,)), ((), ()))


def shift(v, axis, k):
    n = 8 if axis == Z else 4
    return lax.ppermute(v, axis, [(s, (s + k) % n) for s in range(n)])


def parity(info, rows, cols):
    m = (rows * W * INT(MULT) + info[4]) + cols * INT(MULT)
    m = m ^ lax.shift_right_logical(m, INT(16))
    m = m * INT(73244475)
    m = m ^ info[5]
    m = m ^ lax.shift_right_logical(m, INT(15))
    return lax.shift_right_logical(m, INT(9)) & INT(1)


def probe_kernel(info, out):
    x, y = info[0], info[1]
    cols = lax.broadcasted_iota(INT, (1, F), 1) + pl.program_id(0) * F
    rows = lax.broadcasted_iota(INT, (R, 1), 0)
    for zh in range(2):
        d = rows + (x * 8 + zh * 4 + y) * R
        out[zh * R : (zh + 1) * R, :] = (1 - 2 * parity(info, d, cols)).astype(F32).astype(BF16)


def make_probe(info):
    return pl.pallas_call(
        probe_kernel,
        grid=(8,),
        in_specs=[pl.BlockSpec(memory_space=pltpu.SMEM)],
        out_specs=pl.BlockSpec((D, F), lambda j: (0, j)),
        out_shape=jax.ShapeDtypeStruct((D, W), BF16),
        compiler_params=pltpu.CompilerParams(vmem_limit_bytes=16 * MIB),
        cost_estimate=pl.CostEstimate(flops=14 * D * W, bytes_accessed=2 * D * W, transcendentals=0),
    )(info)


def regroup_kernel(info, residual, cotangent, gains, out, gain):
    x, y, c = info[0], info[1], info[3]
    eye = lax.broadcasted_iota(INT, (R, R), 0) == lax.broadcasted_iota(INT, (R, R), 1)
    for zh in range(2):
        row = gains[pl.ds(x * 8 + zh * 4 + y, 1), :]
        gain[zh * R : (zh + 1) * R, :] = jnp.sum(jnp.where(eye, row, 0.0), axis=1, keepdims=True)

    @pl.when(c == 0)
    def _():
        for n, v in enumerate((residual, cotangent)):
            for k in range(4):
                part = v[:, pl.ds(pl.multiple_of((x + k) % 4 * (8 * R), 8 * R), 8 * R)]
                for at in range(4):
                    for zh in range(2):
                        first = at * 2 * D + n * D + zh * R
                        out[k, :, first : first + R] = part[:, (zh * 4 + at) * R : (zh * 4 + at + 1) * R]

    @pl.when(c == 1)
    def _():
        for n, v in enumerate((residual, cotangent)):
            for at in range(4):
                part = v[:, at * 8 * R : (at + 1) * 8 * R]
                for to in range(4):
                    k = (to - y + 4) % 4
                    for zh in range(2):
                        first = at * 2 * D + n * D + zh * R
                        out[k, :, first : first + R] = part[:, (zh * 4 + to) * R : (zh * 4 + to + 1) * R]


def regroup(info, residual, cotangent, norm_gain):
    return pl.pallas_call(
        regroup_kernel,
        in_specs=[pl.BlockSpec(memory_space=pltpu.SMEM)] + [pl.BlockSpec(memory_space=pltpu.VMEM)] * 3,
        out_shape=[jax.ShapeDtypeStruct((4, OWN, 8 * D), BF16), jax.ShapeDtypeStruct((D, 1), F32)],
        compiler_params=pltpu.CompilerParams(vmem_limit_bytes=16 * MIB),
        cost_estimate=pl.CostEstimate(flops=0, bytes_accessed=8 * OWN * N, transcendentals=0),
    )(info, residual, cotangent, norm_gain.reshape(32, R))


def first_kernel(rows, rest, *out):
    for k in range(4):
        for t in range(8):
            out[k][:OWN, t * F : (t + 1) * F] = rows[t]
        out[k][OWN:] = rest[k]


def first_leg(rows, rest):
    return pl.pallas_call(
        first_kernel,
        out_shape=[jax.ShapeDtypeStruct((2 * OWN, W), BF16)] * 4,
        compiler_params=pltpu.CompilerParams(vmem_limit_bytes=16 * MIB),
        cost_estimate=pl.CostEstimate(flops=0, bytes_accessed=32 * OWN * W, transcendentals=0),
    )(rows, rest)


def second_kernel(info, *refs):
    came, out = refs[:4], refs[4:]
    place = jnp.where(info[3] == 0, info[1], info[0])
    for j in range(4):
        columns = pl.ds(pl.multiple_of((place + j) % 4 * 2 * D, 2 * D), 2 * D)
        for k in range(4):
            out[j][k, :, :W] = came[k][:OWN]
            out[j][k, :, W:] = came[k][OWN:, columns]


def second_leg(info, came):
    return pl.pallas_call(
        second_kernel,
        in_specs=[pl.BlockSpec(memory_space=pltpu.SMEM)] + [pl.BlockSpec(memory_space=pltpu.VMEM)] * 4,
        out_shape=[jax.ShapeDtypeStruct((4, OWN, E), BF16)] * 4,
        compiler_params=pltpu.CompilerParams(vmem_limit_bytes=16 * MIB),
        cost_estimate=pl.CostEstimate(flops=0, bytes_accessed=64 * OWN * E, transcendentals=0),
    )(info, *came)


def tangent_kernel(info, *refs):
    pieces, (probe, gain), (context, residual, u_out, w_out), cotangent = refs[:4], refs[4:6], refs[6:10], refs[10]
    x, y, c = info[0], info[1], info[3]
    for j in range(4):
        for k in range(4):
            ax = (x - jnp.where(c == 0, k, j) + 4) % 4
            ay = (y - jnp.where(c == 0, j, k) + 4) % 4
            row = pl.ds(pl.multiple_of((ax * 4 + ay) * OWN, OWN), OWN)
            context[row, :] = pieces[j][k, :, :W]
            residual[row, :] = pieces[j][k, :, W : W + D]
            cotangent[row, :] = pieces[j][k, :, W + D :]
    u_out[...] = lax.dot_general(probe[...], context[...], NT, preferred_element_type=F32)
    w_out[...] = turned(cotangent[...]) * gain[...]


def turned(v):
    eye = (lax.broadcasted_iota(INT, (D, D), 0) == lax.broadcasted_iota(INT, (D, D), 1)).astype(F32).astype(BF16)
    return lax.dot_general(eye, v, NT, preferred_element_type=F32)


def tangent_of(info, pieces, probe, gain):
    return pl.pallas_call(
        tangent_kernel,
        in_specs=[pl.BlockSpec(memory_space=pltpu.SMEM)] + [pl.BlockSpec(memory_space=pltpu.VMEM)] * 6,
        out_shape=[jax.ShapeDtypeStruct((TOK, W), BF16), jax.ShapeDtypeStruct((TOK, D), BF16)]
        + [jax.ShapeDtypeStruct((D, TOK), F32)] * 2,
        scratch_shapes=[pltpu.VMEM((TOK, D), BF16)],
        compiler_params=pltpu.CompilerParams(vmem_limit_bytes=16 * MIB),
        cost_estimate=pl.CostEstimate(flops=2 * D * TOK * W, bytes_accessed=8 * TOK * W, transcendentals=0),
    )(info, *pieces, probe, gain)


def stream_kernel(info, own, other, context, residual, u_in, w_in, s_out, stats, weight):
    zr, c = info[2], info[3]
    for zh in range(2):
        for zl in range(4):
            at = (zr - (zh * 4 + zl) + 8) % 8
            rows = slice(zh * R, (zh + 1) * R)
            weight[rows, pl.ds(pl.multiple_of((zl * 2 + c) * F, F), F)] = own[at]
            weight[rows, pl.ds(pl.multiple_of((zl * 2 + 1 - c) * F, F), F)] = other[at]
    s = turned(residual[...]) + lax.dot_general(weight[...], context[...], NT, preferred_element_type=F32)
    s_out[...] = s
    u, w = u_in[...], w_in[...]
    mean = lambda v: jnp.sum(v, axis=0, keepdims=True) * (1.0 / D)
    ms, mu, mw = mean(s), mean(u), mean(w)
    sc, uc, wc = s - ms, u - mu, w - mw
    stats[0:1] = ms
    stats[1:2] = mu
    stats[2:3] = mw
    stats[3:4] = mean(sc * sc)
    stats[4:5] = mean(sc * uc)
    stats[5:6] = mean(sc * wc)
    stats[6:7] = mean(uc * wc)
    stats[7:8] = jnp.zeros_like(ms)


def stream_of(info, own, other, context, residual, u, w):
    return pl.pallas_call(
        stream_kernel,
        in_specs=[pl.BlockSpec(memory_space=pltpu.SMEM)] + [pl.BlockSpec(memory_space=pltpu.VMEM)] * 6,
        out_shape=[jax.ShapeDtypeStruct((D, TOK), F32), jax.ShapeDtypeStruct((8, TOK), F32)],
        scratch_shapes=[pltpu.VMEM((D, W), BF16)],
        compiler_params=pltpu.CompilerParams(vmem_limit_bytes=16 * MIB),
        cost_estimate=pl.CostEstimate(flops=2 * D * TOK * W, bytes_accessed=8 * TOK * W, transcendentals=0),
    )(info, own, other, context, residual, u, w)


def gradient(stats, s, u, w):
    parts = [stats[j] for j in range(16)]
    total = parts[0]
    for part in parts[1:]:
        total = total + part
    mean = total * (1.0 / 16)
    ms, mu, mw = mean[0:1], mean[1:2], mean[2:3]
    css, csu, csw, cuw = mean[3:4], mean[4:5], mean[5:6], mean[6:7]
    for part in parts:
        ds, du, dw = part[0:1] - ms, part[1:2] - mu, part[2:3] - mw
        css = css + ds * ds * (1.0 / 16)
        csu = csu + ds * du * (1.0 / 16)
        csw = csw + ds * dw * (1.0 / 16)
        cuw = cuw + du * dw * (1.0 / 16)
    r2 = 1.0 / (css + 1e-05)
    r = lax.rsqrt(css + 1e-05)
    k = -(r * r2)
    gamma = cuw - 3.0 * r2 * csu * csw
    value = k * (csu * (w[...] - mw) + csw * (u[...] - mu) + gamma * (s[...] - ms))
    return value.astype(BF16)


def owner(info, k):
    chip = (info[2] + k) % 8
    return pl.ds(pl.multiple_of(chip // 4 * R, R), R), chip % 4 * 2


def away_kernel(info, stats, s, u, w, context, grad, send):
    grad[...] = gradient(stats, s, u, w)
    for k in range(8):
        rows, feature = owner(info, k)
        columns = context[:, pl.ds(pl.multiple_of((feature + 1 - info[3]) * F, F), F)]
        send[k] = jnp.dot(grad[rows, :], columns, preferred_element_type=F32).astype(BF16)


def away(info, stats, s, u, w, context):
    return pl.pallas_call(
        away_kernel,
        in_specs=[pl.BlockSpec(memory_space=pltpu.SMEM)] + [pl.BlockSpec(memory_space=pltpu.VMEM)] * 5,
        out_shape=[jax.ShapeDtypeStruct((D, TOK), BF16), jax.ShapeDtypeStruct((8, R, F), BF16)],
        compiler_params=pltpu.CompilerParams(vmem_limit_bytes=16 * MIB),
        cost_estimate=pl.CostEstimate(flops=D * TOK * W, bytes_accessed=8 * TOK * W, transcendentals=0),
    )(info, stats, s, u, w, context)


def home_kernel(info, grad, context, received, near_up, near_down, three_up, three_down, four_up, four_down, kept):
    def part(k):
        rows, feature = owner(info, k)
        columns = context[:, pl.ds(pl.multiple_of((feature + info[3]) * F, F), F)]
        return jnp.dot(grad[rows, :], columns, preferred_element_type=F32) + received[k].astype(F32)

    three_up[...] = part(3).astype(BF16)
    three_down[...] = part(5).astype(BF16)
    four = part(4).astype(BF16)
    four_up[...] = four[: R // 2]
    four_down[...] = four[R // 2 :]
    near_up[...] = part(1).astype(BF16)
    near_down[...] = part(7).astype(BF16)
    for n, k in enumerate((0, 2, 6)):
        kept[n] = part(k)


def home(info, grad, context, received):
    return pl.pallas_call(
        home_kernel,
        in_specs=[pl.BlockSpec(memory_space=pltpu.SMEM)] + [pl.BlockSpec(memory_space=pltpu.VMEM)] * 3,
        out_shape=[jax.ShapeDtypeStruct((R, F), BF16)] * 4
        + [jax.ShapeDtypeStruct((R // 2, F), BF16)] * 2
        + [jax.ShapeDtypeStruct((3, R, F), F32)],
        compiler_params=pltpu.CompilerParams(vmem_limit_bytes=16 * MIB),
        cost_estimate=pl.CostEstimate(flops=D * TOK * W, bytes_accessed=8 * TOK * W, transcendentals=0),
    )(info, grad, context, received)


def last_kernel(info, kept, a, b, up, down, out):
    rows = lax.broadcasted_iota(INT, (R, 1), 0) + (info[0] * 8 + info[2] // 4 * 4 + info[1]) * R
    cols = lax.broadcasted_iota(INT, (1, F), 1) + (info[2] % 4 * 2 + info[3]) * F
    total = kept[0] + a[...].astype(F32) + b[...].astype(F32) + up[...].astype(F32) + down[...].astype(F32)
    out[...] = jnp.where(parity(info, rows, cols) == 0, total, -total)


def last(info, kept, *parts):
    return pl.pallas_call(
        last_kernel,
        in_specs=[pl.BlockSpec(memory_space=pltpu.SMEM)] + [pl.BlockSpec(memory_space=pltpu.VMEM)] * 5,
        out_shape=jax.ShapeDtypeStruct((R, F), F32),
        compiler_params=pltpu.CompilerParams(vmem_limit_bytes=16 * MIB),
        cost_estimate=pl.CostEstimate(flops=20 * R * F, bytes_accessed=20 * R * F, transcendentals=0),
    )(info, kept, *parts)


def between_kernel(kept, three_up, three_down, four_up, four_down, up, down):
    h = R // 2
    up[:h] = (kept[1, :h] + three_up[:h].astype(F32) + four_up[...].astype(F32)).astype(BF16)
    up[h:] = (kept[1, h:] + three_up[h:].astype(F32)).astype(BF16)
    down[:h] = (kept[2, :h] + three_down[:h].astype(F32)).astype(BF16)
    down[h:] = (kept[2, h:] + three_down[h:].astype(F32) + four_down[...].astype(F32)).astype(BF16)


def between(*parts):
    return pl.pallas_call(
        between_kernel,
        out_shape=[jax.ShapeDtypeStruct((R, F), BF16)] * 2,
        compiler_params=pltpu.CompilerParams(vmem_limit_bytes=16 * MIB),
        cost_estimate=pl.CostEstimate(flops=8 * R * F, bytes_accessed=20 * R * F, transcendentals=0),
    )(*parts)


def swap(v):
    return lax.ppermute(v, "c", [(0, 1), (1, 0)])


def after(v, *others):
    return lax.optimization_barrier((v, *others))[0]


def leg(blocks, axes):
    out = [blocks[0]]
    for k in range(1, 4):
        pairs = []
        for x in range(4):
            for y in range(4):
                for c in range(2):
                    to = ((x + k) % 4, y) if axes[c] == "x" else (x, (y + k) % 4)
                    pairs.append(((x * 4 + y) * 2 + c, (to[0] * 4 + to[1]) * 2 + c))
        out.append(lax.ppermute(blocks[k], XYC, pairs))
    return out


def on_device(context, residual, out_proj, norm_gain, cotangent, probe_seed):
    x, zh, y, zl, c = (lax.axis_index(a).astype(INT) for a in AXES)
    info = jnp.concatenate([jnp.stack([x, y, zh * 4 + zl, c]), probe_seed])

    rest, gain = regroup(info, residual, cotangent, norm_gain)
    rows = lax.all_to_all(context.reshape(8, OWN, F), T, 0, 0, tiled=True)
    rows, rest, gain = lax.optimization_barrier((rows, rest, gain))

    came = lax.optimization_barrier(leg(first_leg(rows, rest), "xy"))
    behind, ahead = shift(out_proj, Z, 1), shift(out_proj, Z, -1)
    two, ahead2 = after(jnp.stack([out_proj, behind]), rows), after(jnp.stack([out_proj, ahead]), rows)
    behind2, ahead2 = shift(two, Z, 2), shift(ahead2, Z, -2)
    far = shift(after(ahead2[1], *came), Z, -1)
    own = jnp.concatenate([two, behind2, far[None], ahead2[::-1], ahead[None]])

    probe = make_probe(after(info, *came))
    *pieces, probe, own = lax.optimization_barrier((*leg(second_leg(info, came), "yx"), probe, own))
    other = swap(own)
    rows, res, u, w = tangent_of(info, pieces, probe, gain)
    s, stats = stream_of(info, own, other, rows, res, u, w)
    stats = lax.all_to_all(jnp.broadcast_to(stats[None], (16, 8, TOK)), XY, 0, 0, tiled=True)
    grad, send = away(info, stats, s, u, w, rows)
    near_up, near_down, three_up, three_down, four_up, four_down, kept = home(info, grad, rows, swap(send))

    near_up, near_down = shift(near_up, Z, 1), shift(near_down, Z, -1)
    three_up, three_down = shift(three_up, Z, 1), shift(three_down, Z, -1)
    four_up, four_down = shift(four_up, Z, 2), shift(four_down, Z, -2)
    up, down = between(kept, three_up, three_down, four_up, four_down)
    up, down = shift(up, Z, 2), shift(down, Z, -2)
    return last(info, kept, near_up, near_down, up, down)


def solution(mesh):
    split = Mesh(mesh.devices.reshape(GRID), AXES)
    dp, tensor = ("x", "zh", "y"), T
    in_specs = (
        P(dp, tensor),
        P((*dp, *tensor), None),
        P(dp, tensor),
        P(),
        P((*dp, *tensor), None),
        P(),
    )
    return jax.shard_map(on_device, mesh=split, in_specs=in_specs, out_specs=P(dp, tensor), check_vma=False)
```

```python
import jax
import jax.numpy as jnp
from jax import lax
from jax.experimental import pallas as pl
from jax.experimental.pallas import tpu as pltpu
from jax.sharding import Mesh
from jax.sharding import PartitionSpec as P

AXES = ("x", "zh", "y", "zl", "c")
GRID = (4, 2, 4, 4, 2)
Z = ("zh", "zl")
XY = ("x", "y")
T = ("zl", "c")
R = 192
F = 384
W = 8 * F
OWN = 32
TOK = 16 * OWN
D = 2 * R
N = 32 * R
E = W + 2 * D
XYC = ("x", "y", "c")
MIB = 1024 * 1024
MULT = 747796405
INT = jnp.int32
F32 = jnp.float32
BF16 = jnp.bfloat16
NT = (((1,), (1,)), ((), ()))


def shift(v, axis, k):
    n = 8 if axis == Z else 4
    return lax.ppermute(v, axis, [(s, (s + k) % n) for s in range(n)])


def parity(info, rows, cols):
    m = (rows * W * INT(MULT) + info[4]) + cols * INT(MULT)
    m = m ^ lax.shift_right_logical(m, INT(16))
    m = m * INT(73244475)
    m = m ^ info[5]
    m = m ^ lax.shift_right_logical(m, INT(15))
    return lax.shift_right_logical(m, INT(9)) & INT(1)


def probe_kernel(info, out):
    x, y = info[0], info[1]
    cols = lax.broadcasted_iota(INT, (1, F), 1) + pl.program_id(0) * F
    rows = lax.broadcasted_iota(INT, (R, 1), 0)
    for zh in range(2):
        d = rows + (x * 8 + zh * 4 + y) * R
        out[zh * R : (zh + 1) * R, :] = (1 - 2 * parity(info, d, cols)).astype(F32).astype(BF16)


def make_probe(info):
    return pl.pallas_call(
        probe_kernel,
        grid=(8,),
        in_specs=[pl.BlockSpec(memory_space=pltpu.SMEM)],
        out_specs=pl.BlockSpec((D, F), lambda j: (0, j)),
        out_shape=jax.ShapeDtypeStruct((D, W), BF16),
        compiler_params=pltpu.CompilerParams(vmem_limit_bytes=16 * MIB),
        cost_estimate=pl.CostEstimate(flops=14 * D * W, bytes_accessed=2 * D * W, transcendentals=0),
    )(info)


def regroup_kernel(info, residual, cotangent, gains, out, gain):
    x, y, c = info[0], info[1], info[3]
    eye = lax.broadcasted_iota(INT, (R, R), 0) == lax.broadcasted_iota(INT, (R, R), 1)
    for zh in range(2):
        row = gains[pl.ds(x * 8 + zh * 4 + y, 1), :]
        gain[zh * R : (zh + 1) * R, :] = jnp.sum(jnp.where(eye, row, 0.0), axis=1, keepdims=True)

    @pl.when(c == 0)
    def _():
        for n, v in enumerate((residual, cotangent)):
            for k in range(4):
                part = v[:, pl.ds(pl.multiple_of((x + k) % 4 * (8 * R), 8 * R), 8 * R)]
                for at in range(4):
                    for zh in range(2):
                        first = at * 2 * D + n * D + zh * R
                        out[k, :, first : first + R] = part[:, (zh * 4 + at) * R : (zh * 4 + at + 1) * R]

    @pl.when(c == 1)
    def _():
        for n, v in enumerate((residual, cotangent)):
            for at in range(4):
                part = v[:, at * 8 * R : (at + 1) * 8 * R]
                for to in range(4):
                    k = (to - y + 4) % 4
                    for zh in range(2):
                        first = at * 2 * D + n * D + zh * R
                        out[k, :, first : first + R] = part[:, (zh * 4 + to) * R : (zh * 4 + to + 1) * R]


def regroup(info, residual, cotangent, norm_gain):
    return pl.pallas_call(
        regroup_kernel,
        in_specs=[pl.BlockSpec(memory_space=pltpu.SMEM)] + [pl.BlockSpec(memory_space=pltpu.VMEM)] * 3,
        out_shape=[jax.ShapeDtypeStruct((4, OWN, 8 * D), BF16), jax.ShapeDtypeStruct((D, 1), F32)],
        compiler_params=pltpu.CompilerParams(vmem_limit_bytes=16 * MIB),
        cost_estimate=pl.CostEstimate(flops=0, bytes_accessed=8 * OWN * N, transcendentals=0),
    )(info, residual, cotangent, norm_gain.reshape(32, R))


def first_kernel(rows, rest, *out):
    for k in range(4):
        for t in range(8):
            out[k][:OWN, t * F : (t + 1) * F] = rows[t]
        out[k][OWN:] = rest[k]


def first_leg(rows, rest):
    return pl.pallas_call(
        first_kernel,
        out_shape=[jax.ShapeDtypeStruct((2 * OWN, W), BF16)] * 4,
        compiler_params=pltpu.CompilerParams(vmem_limit_bytes=16 * MIB),
        cost_estimate=pl.CostEstimate(flops=0, bytes_accessed=32 * OWN * W, transcendentals=0),
    )(rows, rest)


def second_kernel(info, *refs):
    came, out = refs[:4], refs[4:]
    place = jnp.where(info[3] == 0, info[1], info[0])
    for j in range(4):
        columns = pl.ds(pl.multiple_of((place + j) % 4 * 2 * D, 2 * D), 2 * D)
        for k in range(4):
            out[j][k, :, :W] = came[k][:OWN]
            out[j][k, :, W:] = came[k][OWN:, columns]


def second_leg(info, came):
    return pl.pallas_call(
        second_kernel,
        in_specs=[pl.BlockSpec(memory_space=pltpu.SMEM)] + [pl.BlockSpec(memory_space=pltpu.VMEM)] * 4,
        out_shape=[jax.ShapeDtypeStruct((4, OWN, E), BF16)] * 4,
        compiler_params=pltpu.CompilerParams(vmem_limit_bytes=16 * MIB),
        cost_estimate=pl.CostEstimate(flops=0, bytes_accessed=64 * OWN * E, transcendentals=0),
    )(info, *came)


def tangent_kernel(info, *refs):
    pieces, (probe, gain), (context, residual, u_out, w_out), cotangent = refs[:4], refs[4:6], refs[6:10], refs[10]
    x, y, c = info[0], info[1], info[3]
    for j in range(4):
        for k in range(4):
            ax = (x - jnp.where(c == 0, k, j) + 4) % 4
            ay = (y - jnp.where(c == 0, j, k) + 4) % 4
            row = pl.ds(pl.multiple_of((ax * 4 + ay) * OWN, OWN), OWN)
            context[row, :] = pieces[j][k, :, :W]
            residual[row, :] = pieces[j][k, :, W : W + D]
            cotangent[row, :] = pieces[j][k, :, W + D :]
    u_out[...] = lax.dot_general(probe[...], context[...], NT, preferred_element_type=F32)
    w_out[...] = turned(cotangent[...]) * gain[...]


def turned(v):
    eye = (lax.broadcasted_iota(INT, (D, D), 0) == lax.broadcasted_iota(INT, (D, D), 1)).astype(F32).astype(BF16)
    return lax.dot_general(eye, v, NT, preferred_element_type=F32)


def tangent_of(info, pieces, probe, gain):
    return pl.pallas_call(
        tangent_kernel,
        in_specs=[pl.BlockSpec(memory_space=pltpu.SMEM)] + [pl.BlockSpec(memory_space=pltpu.VMEM)] * 6,
        out_shape=[jax.ShapeDtypeStruct((TOK, W), BF16), jax.ShapeDtypeStruct((TOK, D), BF16)]
        + [jax.ShapeDtypeStruct((D, TOK), F32)] * 2,
        scratch_shapes=[pltpu.VMEM((TOK, D), BF16)],
        compiler_params=pltpu.CompilerParams(vmem_limit_bytes=16 * MIB),
        cost_estimate=pl.CostEstimate(flops=2 * D * TOK * W, bytes_accessed=8 * TOK * W, transcendentals=0),
    )(info, *pieces, probe, gain)


def stream_kernel(info, own, other, context, residual, u_in, w_in, s_out, stats, weight):
    zr, c = info[2], info[3]
    for zh in range(2):
        for zl in range(4):
            at = (zr - (zh * 4 + zl) + 8) % 8
            rows = slice(zh * R, (zh + 1) * R)
            weight[rows, pl.ds(pl.multiple_of((zl * 2 + c) * F, F), F)] = own[at]
            weight[rows, pl.ds(pl.multiple_of((zl * 2 + 1 - c) * F, F), F)] = other[at]
    s = turned(residual[...]) + lax.dot_general(weight[...], context[...], NT, preferred_element_type=F32)
    s_out[...] = s
    u, w = u_in[...], w_in[...]
    mean = lambda v: jnp.sum(v, axis=0, keepdims=True) * (1.0 / D)
    ms, mu, mw = mean(s), mean(u), mean(w)
    sc, uc, wc = s - ms, u - mu, w - mw
    stats[0:1] = ms
    stats[1:2] = mu
    stats[2:3] = mw
    stats[3:4] = mean(sc * sc)
    stats[4:5] = mean(sc * uc)
    stats[5:6] = mean(sc * wc)
    stats[6:7] = mean(uc * wc)
    stats[7:8] = jnp.zeros_like(ms)


def stream_of(info, own, other, context, residual, u, w):
    return pl.pallas_call(
        stream_kernel,
        in_specs=[pl.BlockSpec(memory_space=pltpu.SMEM)] + [pl.BlockSpec(memory_space=pltpu.VMEM)] * 6,
        out_shape=[jax.ShapeDtypeStruct((D, TOK), F32), jax.ShapeDtypeStruct((8, TOK), F32)],
        scratch_shapes=[pltpu.VMEM((D, W), BF16)],
        compiler_params=pltpu.CompilerParams(vmem_limit_bytes=16 * MIB),
        cost_estimate=pl.CostEstimate(flops=2 * D * TOK * W, bytes_accessed=8 * TOK * W, transcendentals=0),
    )(info, own, other, context, residual, u, w)


def gradient(stats, s, u, w):
    parts = [stats[j] for j in range(16)]
    total = parts[0]
    for part in parts[1:]:
        total = total + part
    mean = total * (1.0 / 16)
    ms, mu, mw = mean[0:1], mean[1:2], mean[2:3]
    css, csu, csw, cuw = mean[3:4], mean[4:5], mean[5:6], mean[6:7]
    for part in parts:
        ds, du, dw = part[0:1] - ms, part[1:2] - mu, part[2:3] - mw
        css = css + ds * ds * (1.0 / 16)
        csu = csu + ds * du * (1.0 / 16)
        csw = csw + ds * dw * (1.0 / 16)
        cuw = cuw + du * dw * (1.0 / 16)
    r2 = 1.0 / (css + 1e-05)
    r = lax.rsqrt(css + 1e-05)
    k = -(r * r2)
    gamma = cuw - 3.0 * r2 * csu * csw
    value = k * (csu * (w[...] - mw) + csw * (u[...] - mu) + gamma * (s[...] - ms))
    return value.astype(BF16)


def owner(info, k):
    chip = (info[2] + k) % 8
    return pl.ds(pl.multiple_of(chip // 4 * R, R), R), chip % 4 * 2


def away_kernel(info, stats, s, u, w, context, grad, send):
    grad[...] = gradient(stats, s, u, w)
    for k in range(8):
        rows, feature = owner(info, k)
        columns = context[:, pl.ds(pl.multiple_of((feature + 1 - info[3]) * F, F), F)]
        send[k] = jnp.dot(grad[rows, :], columns, preferred_element_type=F32).astype(BF16)


def away(info, stats, s, u, w, context):
    return pl.pallas_call(
        away_kernel,
        in_specs=[pl.BlockSpec(memory_space=pltpu.SMEM)] + [pl.BlockSpec(memory_space=pltpu.VMEM)] * 5,
        out_shape=[jax.ShapeDtypeStruct((D, TOK), BF16), jax.ShapeDtypeStruct((8, R, F), BF16)],
        compiler_params=pltpu.CompilerParams(vmem_limit_bytes=16 * MIB),
        cost_estimate=pl.CostEstimate(flops=D * TOK * W, bytes_accessed=8 * TOK * W, transcendentals=0),
    )(info, stats, s, u, w, context)


def home_kernel(info, grad, context, received, near_up, near_down, three_up, three_down, four_up, four_down, kept):
    def part(k):
        rows, feature = owner(info, k)
        columns = context[:, pl.ds(pl.multiple_of((feature + info[3]) * F, F), F)]
        return jnp.dot(grad[rows, :], columns, preferred_element_type=F32) + received[k].astype(F32)

    three_up[...] = part(3).astype(BF16)
    three_down[...] = part(5).astype(BF16)
    four = part(4).astype(BF16)
    four_up[...] = four[: R // 2]
    four_down[...] = four[R // 2 :]
    near_up[...] = part(1).astype(BF16)
    near_down[...] = part(7).astype(BF16)
    for n, k in enumerate((0, 2, 6)):
        kept[n] = part(k)


def home(info, grad, context, received):
    return pl.pallas_call(
        home_kernel,
        in_specs=[pl.BlockSpec(memory_space=pltpu.SMEM)] + [pl.BlockSpec(memory_space=pltpu.VMEM)] * 3,
        out_shape=[jax.ShapeDtypeStruct((R, F), BF16)] * 4
        + [jax.ShapeDtypeStruct((R // 2, F), BF16)] * 2
        + [jax.ShapeDtypeStruct((3, R, F), F32)],
        compiler_params=pltpu.CompilerParams(vmem_limit_bytes=16 * MIB),
        cost_estimate=pl.CostEstimate(flops=D * TOK * W, bytes_accessed=8 * TOK * W, transcendentals=0),
    )(info, grad, context, received)


def last_kernel(info, kept, a, b, up, down, out):
    rows = lax.broadcasted_iota(INT, (R, 1), 0) + (info[0] * 8 + info[2] // 4 * 4 + info[1]) * R
    cols = lax.broadcasted_iota(INT, (1, F), 1) + (info[2] % 4 * 2 + info[3]) * F
    total = kept[0] + a[...].astype(F32) + b[...].astype(F32) + up[...].astype(F32) + down[...].astype(F32)
    out[...] = jnp.where(parity(info, rows, cols) == 0, total, -total)


def last(info, kept, *parts):
    return pl.pallas_call(
        last_kernel,
        in_specs=[pl.BlockSpec(memory_space=pltpu.SMEM)] + [pl.BlockSpec(memory_space=pltpu.VMEM)] * 5,
        out_shape=jax.ShapeDtypeStruct((R, F), F32),
        compiler_params=pltpu.CompilerParams(vmem_limit_bytes=16 * MIB),
        cost_estimate=pl.CostEstimate(flops=20 * R * F, bytes_accessed=20 * R * F, transcendentals=0),
    )(info, kept, *parts)


def between_kernel(kept, three_up, three_down, four_up, four_down, up, down):
    h = R // 2
    up[:h] = (kept[1, :h] + three_up[:h].astype(F32) + four_up[...].astype(F32)).astype(BF16)
    up[h:] = (kept[1, h:] + three_up[h:].astype(F32)).astype(BF16)
    down[:h] = (kept[2, :h] + three_down[:h].astype(F32)).astype(BF16)
    down[h:] = (kept[2, h:] + three_down[h:].astype(F32) + four_down[...].astype(F32)).astype(BF16)


def between(*parts):
    return pl.pallas_call(
        between_kernel,
        out_shape=[jax.ShapeDtypeStruct((R, F), BF16)] * 2,
        compiler_params=pltpu.CompilerParams(vmem_limit_bytes=16 * MIB),
        cost_estimate=pl.CostEstimate(flops=8 * R * F, bytes_accessed=20 * R * F, transcendentals=0),
    )(*parts)


def swap(v):
    return lax.ppermute(v, "c", [(0, 1), (1, 0)])


def after(v, *others):
    return lax.optimization_barrier((v, *others))[0]


def leg(blocks, axes):
    out = [blocks[0]]
    for k in (1, 3, 2):
        pairs = []
        for x in range(4):
            for y in range(4):
                for c in range(2):
                    to = ((x + k) % 4, y) if axes[c] == "x" else (x, (y + k) % 4)
                    pairs.append(((x * 4 + y) * 2 + c, (to[0] * 4 + to[1]) * 2 + c))
        out.append(lax.ppermute(blocks[k], XYC, pairs))
    return out


def on_device(context, residual, out_proj, norm_gain, cotangent, probe_seed):
    x, zh, y, zl, c = (lax.axis_index(a).astype(INT) for a in AXES)
    info = jnp.concatenate([jnp.stack([x, y, zh * 4 + zl, c]), probe_seed])

    rest, gain = regroup(info, residual, cotangent, norm_gain)
    rows = lax.all_to_all(context.reshape(8, OWN, F), T, 0, 0, tiled=True)
    rows, rest, gain = lax.optimization_barrier((rows, rest, gain))

    came = lax.optimization_barrier(leg(first_leg(rows, rest), "xy"))
    came = [came[n] for n in (0, 1, 3, 2)]
    behind, ahead = shift(out_proj, Z, 1), shift(out_proj, Z, -1)
    two, ahead2 = after(jnp.stack([out_proj, behind]), rows), after(jnp.stack([out_proj, ahead]), rows)
    behind2, ahead2 = shift(two, Z, 2), shift(ahead2, Z, -2)
    far = shift(after(ahead2[1], *came), Z, -1)
    own = jnp.concatenate([two, behind2, far[None], ahead2[::-1], ahead[None]])

    probe = make_probe(after(info, *came))
    *pieces, probe, own = lax.optimization_barrier((*leg(second_leg(info, came), "yx"), probe, own))
    pieces = [pieces[n] for n in (0, 1, 3, 2)]
    other = swap(own)
    rows, res, u, w = tangent_of(info, pieces, probe, gain)
    s, stats = stream_of(info, own, other, rows, res, u, w)
    stats = lax.all_to_all(jnp.broadcast_to(stats[None], (16, 8, TOK)), XY, 0, 0, tiled=True)
    grad, send = away(info, stats, s, u, w, rows)
    near_up, near_down, three_up, three_down, four_up, four_down, kept = home(info, grad, rows, swap(send))

    three_up, three_down = shift(three_up, Z, 1), shift(three_down, Z, -1)
    four_up, four_down = shift(four_up, Z, 2), shift(four_down, Z, -2)
    near_up, near_down = shift(near_up, Z, 1), shift(near_down, Z, -1)
    up, down = between(kept, three_up, three_down, four_up, four_down)
    up, down = shift(up, Z, 2), shift(down, Z, -2)
    return last(info, kept, near_up, near_down, up, down)


def solution(mesh):
    split = Mesh(mesh.devices.reshape(GRID), AXES)
    dp, tensor = ("x", "zh", "y"), T
    in_specs = (
        P(dp, tensor),
        P((*dp, *tensor), None),
        P(dp, tensor),
        P(),
        P((*dp, *tensor), None),
        P(),
    )
    return jax.shard_map(on_device, mesh=split, in_specs=in_specs, out_specs=P(dp, tensor), check_vma=False)
```

```python
import jax
import jax.numpy as jnp
from jax import lax
from jax.experimental import pallas as pl
from jax.experimental.pallas import tpu as pltpu
from jax.sharding import Mesh
from jax.sharding import PartitionSpec as P

AXES = ("x", "zh", "y", "zl", "c")
GRID = (4, 2, 4, 4, 2)
Z = ("zh", "zl")
XY = ("x", "y")
T = ("zl", "c")
R = 192
F = 384
W = 8 * F
OWN = 32
TOK = 16 * OWN
D = 2 * R
N = 32 * R
E = W + 2 * D
XYC = ("x", "y", "c")
MIB = 1024 * 1024
MULT = 747796405
INT = jnp.int32
F32 = jnp.float32
BF16 = jnp.bfloat16
NT = (((1,), (1,)), ((), ()))


def shift(v, axis, k):
    n = 8 if axis == Z else 4
    return lax.ppermute(v, axis, [(s, (s + k) % n) for s in range(n)])


def parity(info, rows, cols):
    m = (rows * W * INT(MULT) + info[4]) + cols * INT(MULT)
    m = m ^ lax.shift_right_logical(m, INT(16))
    m = m * INT(73244475)
    m = m ^ info[5]
    m = m ^ lax.shift_right_logical(m, INT(15))
    return lax.shift_right_logical(m, INT(9)) & INT(1)


def probe_kernel(info, out):
    x, y = info[0], info[1]
    cols = lax.broadcasted_iota(INT, (1, F), 1) + pl.program_id(0) * F
    rows = lax.broadcasted_iota(INT, (R, 1), 0)
    for zh in range(2):
        d = rows + (x * 8 + zh * 4 + y) * R
        out[zh * R : (zh + 1) * R, :] = (1 - 2 * parity(info, d, cols)).astype(F32).astype(BF16)


def make_probe(info):
    return pl.pallas_call(
        probe_kernel,
        grid=(8,),
        in_specs=[pl.BlockSpec(memory_space=pltpu.SMEM)],
        out_specs=pl.BlockSpec((D, F), lambda j: (0, j)),
        out_shape=jax.ShapeDtypeStruct((D, W), BF16),
        compiler_params=pltpu.CompilerParams(vmem_limit_bytes=16 * MIB),
        cost_estimate=pl.CostEstimate(flops=14 * D * W, bytes_accessed=2 * D * W, transcendentals=0),
    )(info)


def regroup_kernel(info, residual, cotangent, gains, out, gain):
    x, y, c = info[0], info[1], info[3]
    eye = lax.broadcasted_iota(INT, (R, R), 0) == lax.broadcasted_iota(INT, (R, R), 1)
    for zh in range(2):
        row = gains[pl.ds(x * 8 + zh * 4 + y, 1), :]
        gain[zh * R : (zh + 1) * R, :] = jnp.sum(jnp.where(eye, row, 0.0), axis=1, keepdims=True)

    @pl.when(c == 0)
    def _():
        for n, v in enumerate((residual, cotangent)):
            for k in range(4):
                part = v[:, pl.ds(pl.multiple_of((x + k) % 4 * (8 * R), 8 * R), 8 * R)]
                for at in range(4):
                    for zh in range(2):
                        first = at * 2 * D + n * D + zh * R
                        out[k, :, first : first + R] = part[:, (zh * 4 + at) * R : (zh * 4 + at + 1) * R]

    @pl.when(c == 1)
    def _():
        for n, v in enumerate((residual, cotangent)):
            for at in range(4):
                part = v[:, at * 8 * R : (at + 1) * 8 * R]
                for to in range(4):
                    k = (to - y + 4) % 4
                    for zh in range(2):
                        first = at * 2 * D + n * D + zh * R
                        out[k, :, first : first + R] = part[:, (zh * 4 + to) * R : (zh * 4 + to + 1) * R]


def regroup(info, residual, cotangent, norm_gain):
    return pl.pallas_call(
        regroup_kernel,
        in_specs=[pl.BlockSpec(memory_space=pltpu.SMEM)] + [pl.BlockSpec(memory_space=pltpu.VMEM)] * 3,
        out_shape=[jax.ShapeDtypeStruct((4, OWN, 8 * D), BF16), jax.ShapeDtypeStruct((D, 1), F32)],
        compiler_params=pltpu.CompilerParams(vmem_limit_bytes=16 * MIB),
        cost_estimate=pl.CostEstimate(flops=0, bytes_accessed=8 * OWN * N, transcendentals=0),
    )(info, residual, cotangent, norm_gain.reshape(32, R))


def first_kernel(rows, rest, *out):
    for k in range(4):
        for t in range(8):
            out[k][:OWN, t * F : (t + 1) * F] = rows[t]
        out[k][OWN:] = rest[k]


def first_leg(rows, rest):
    return pl.pallas_call(
        first_kernel,
        out_shape=[jax.ShapeDtypeStruct((2 * OWN, W), BF16)] * 4,
        compiler_params=pltpu.CompilerParams(vmem_limit_bytes=16 * MIB),
        cost_estimate=pl.CostEstimate(flops=0, bytes_accessed=32 * OWN * W, transcendentals=0),
    )(rows, rest)


def second_kernel(info, *refs):
    came, out = refs[:4], refs[4:]
    place = jnp.where(info[3] == 0, info[1], info[0])
    for j in range(4):
        columns = pl.ds(pl.multiple_of((place + j) % 4 * 2 * D, 2 * D), 2 * D)
        for k in range(4):
            out[j][k, :, :W] = came[k][:OWN]
            out[j][k, :, W:] = came[k][OWN:, columns]


def second_leg(info, came):
    return pl.pallas_call(
        second_kernel,
        in_specs=[pl.BlockSpec(memory_space=pltpu.SMEM)] + [pl.BlockSpec(memory_space=pltpu.VMEM)] * 4,
        out_shape=[jax.ShapeDtypeStruct((4, OWN, E), BF16)] * 4,
        compiler_params=pltpu.CompilerParams(vmem_limit_bytes=16 * MIB),
        cost_estimate=pl.CostEstimate(flops=0, bytes_accessed=64 * OWN * E, transcendentals=0),
    )(info, *came)


def tangent_kernel(info, *refs):
    pieces, (probe, gain), (context, residual, u_out, w_out), cotangent = refs[:4], refs[4:6], refs[6:10], refs[10]
    x, y, c = info[0], info[1], info[3]
    for j in range(4):
        for k in range(4):
            ax = (x - jnp.where(c == 0, k, j) + 4) % 4
            ay = (y - jnp.where(c == 0, j, k) + 4) % 4
            row = pl.ds(pl.multiple_of((ax * 4 + ay) * OWN, OWN), OWN)
            context[row, :] = pieces[j][k, :, :W]
            residual[row, :] = pieces[j][k, :, W : W + D]
            cotangent[row, :] = pieces[j][k, :, W + D :]
    u_out[...] = lax.dot_general(probe[...], context[...], NT, preferred_element_type=F32)
    w_out[...] = turned(cotangent[...]) * gain[...]


def turned(v):
    eye = (lax.broadcasted_iota(INT, (D, D), 0) == lax.broadcasted_iota(INT, (D, D), 1)).astype(F32).astype(BF16)
    return lax.dot_general(eye, v, NT, preferred_element_type=F32)


def tangent_of(info, pieces, probe, gain):
    return pl.pallas_call(
        tangent_kernel,
        in_specs=[pl.BlockSpec(memory_space=pltpu.SMEM)] + [pl.BlockSpec(memory_space=pltpu.VMEM)] * 6,
        out_shape=[jax.ShapeDtypeStruct((TOK, W), BF16), jax.ShapeDtypeStruct((TOK, D), BF16)]
        + [jax.ShapeDtypeStruct((D, TOK), F32)] * 2,
        scratch_shapes=[pltpu.VMEM((TOK, D), BF16)],
        compiler_params=pltpu.CompilerParams(vmem_limit_bytes=16 * MIB),
        cost_estimate=pl.CostEstimate(flops=2 * D * TOK * W, bytes_accessed=8 * TOK * W, transcendentals=0),
    )(info, *pieces, probe, gain)


def stream_kernel(info, own, other, context, residual, u_in, w_in, s_out, stats, weight):
    zr, c = info[2], info[3]
    for zh in range(2):
        for zl in range(4):
            at = (zr - (zh * 4 + zl) + 8) % 8
            rows = slice(zh * R, (zh + 1) * R)
            weight[rows, pl.ds(pl.multiple_of((zl * 2 + c) * F, F), F)] = own[at]
            weight[rows, pl.ds(pl.multiple_of((zl * 2 + 1 - c) * F, F), F)] = other[at]
    s = turned(residual[...]) + lax.dot_general(weight[...], context[...], NT, preferred_element_type=F32)
    s_out[...] = s
    u, w = u_in[...], w_in[...]
    mean = lambda v: jnp.sum(v, axis=0, keepdims=True) * (1.0 / D)
    ms, mu, mw = mean(s), mean(u), mean(w)
    sc, uc, wc = s - ms, u - mu, w - mw
    stats[0:1] = ms
    stats[1:2] = mu
    stats[2:3] = mw
    stats[3:4] = mean(sc * sc)
    stats[4:5] = mean(sc * uc)
    stats[5:6] = mean(sc * wc)
    stats[6:7] = mean(uc * wc)
    stats[7:8] = jnp.zeros_like(ms)


def stream_of(info, own, other, context, residual, u, w):
    return pl.pallas_call(
        stream_kernel,
        in_specs=[pl.BlockSpec(memory_space=pltpu.SMEM)] + [pl.BlockSpec(memory_space=pltpu.VMEM)] * 6,
        out_shape=[jax.ShapeDtypeStruct((D, TOK), F32), jax.ShapeDtypeStruct((8, TOK), F32)],
        scratch_shapes=[pltpu.VMEM((D, W), BF16)],
        compiler_params=pltpu.CompilerParams(vmem_limit_bytes=16 * MIB),
        cost_estimate=pl.CostEstimate(flops=2 * D * TOK * W, bytes_accessed=8 * TOK * W, transcendentals=0),
    )(info, own, other, context, residual, u, w)


def gradient(stats, s, u, w):
    parts = [stats[j] for j in range(16)]
    total = parts[0]
    for part in parts[1:]:
        total = total + part
    mean = total * (1.0 / 16)
    ms, mu, mw = mean[0:1], mean[1:2], mean[2:3]
    css, csu, csw, cuw = mean[3:4], mean[4:5], mean[5:6], mean[6:7]
    for part in parts:
        ds, du, dw = part[0:1] - ms, part[1:2] - mu, part[2:3] - mw
        css = css + ds * ds * (1.0 / 16)
        csu = csu + ds * du * (1.0 / 16)
        csw = csw + ds * dw * (1.0 / 16)
        cuw = cuw + du * dw * (1.0 / 16)
    r2 = 1.0 / (css + 1e-05)
    r = lax.rsqrt(css + 1e-05)
    k = -(r * r2)
    gamma = cuw - 3.0 * r2 * csu * csw
    value = k * (csu * (w[...] - mw) + csw * (u[...] - mu) + gamma * (s[...] - ms))
    return value.astype(BF16)


def owner(info, k):
    chip = (info[2] + k) % 8
    return pl.ds(pl.multiple_of(chip // 4 * R, R), R), chip % 4 * 2


def away_kernel(info, stats, s, u, w, context, grad, send):
    grad[...] = gradient(stats, s, u, w)
    for k in range(8):
        rows, feature = owner(info, k)
        columns = context[:, pl.ds(pl.multiple_of((feature + 1 - info[3]) * F, F), F)]
        send[k] = jnp.dot(grad[rows, :], columns, preferred_element_type=F32).astype(BF16)


def away(info, stats, s, u, w, context):
    return pl.pallas_call(
        away_kernel,
        in_specs=[pl.BlockSpec(memory_space=pltpu.SMEM)] + [pl.BlockSpec(memory_space=pltpu.VMEM)] * 5,
        out_shape=[jax.ShapeDtypeStruct((D, TOK), BF16), jax.ShapeDtypeStruct((8, R, F), BF16)],
        compiler_params=pltpu.CompilerParams(vmem_limit_bytes=16 * MIB),
        cost_estimate=pl.CostEstimate(flops=D * TOK * W, bytes_accessed=8 * TOK * W, transcendentals=0),
    )(info, stats, s, u, w, context)


def home_kernel(info, grad, context, received, near_up, near_down, three_up, three_down, four_up, four_down, kept):
    def part(k):
        rows, feature = owner(info, k)
        columns = context[:, pl.ds(pl.multiple_of((feature + info[3]) * F, F), F)]
        return jnp.dot(grad[rows, :], columns, preferred_element_type=F32) + received[k].astype(F32)

    three_up[...] = part(3).astype(BF16)
    three_down[...] = part(5).astype(BF16)
    four = part(4).astype(BF16)
    four_up[...] = four[: R // 2]
    four_down[...] = four[R // 2 :]
    near_up[...] = part(1).astype(BF16)
    near_down[...] = part(7).astype(BF16)
    for n, k in enumerate((0, 2, 6)):
        kept[n] = part(k)


def home(info, grad, context, received):
    return pl.pallas_call(
        home_kernel,
        in_specs=[pl.BlockSpec(memory_space=pltpu.SMEM)] + [pl.BlockSpec(memory_space=pltpu.VMEM)] * 3,
        out_shape=[jax.ShapeDtypeStruct((R, F), BF16)] * 4
        + [jax.ShapeDtypeStruct((R // 2, F), BF16)] * 2
        + [jax.ShapeDtypeStruct((3, R, F), F32)],
        compiler_params=pltpu.CompilerParams(vmem_limit_bytes=16 * MIB),
        cost_estimate=pl.CostEstimate(flops=D * TOK * W, bytes_accessed=8 * TOK * W, transcendentals=0),
    )(info, grad, context, received)


def last_kernel(info, kept, a, b, up, down, out):
    rows = lax.broadcasted_iota(INT, (R, 1), 0) + (info[0] * 8 + info[2] // 4 * 4 + info[1]) * R
    cols = lax.broadcasted_iota(INT, (1, F), 1) + (info[2] % 4 * 2 + info[3]) * F
    total = kept[0] + a[...].astype(F32) + b[...].astype(F32) + up[...].astype(F32) + down[...].astype(F32)
    out[...] = jnp.where(parity(info, rows, cols) == 0, total, -total)


def last(info, kept, *parts):
    return pl.pallas_call(
        last_kernel,
        in_specs=[pl.BlockSpec(memory_space=pltpu.SMEM)] + [pl.BlockSpec(memory_space=pltpu.VMEM)] * 5,
        out_shape=jax.ShapeDtypeStruct((R, F), F32),
        compiler_params=pltpu.CompilerParams(vmem_limit_bytes=16 * MIB),
        cost_estimate=pl.CostEstimate(flops=20 * R * F, bytes_accessed=20 * R * F, transcendentals=0),
    )(info, kept, *parts)


def between_kernel(kept, three_up, three_down, four_up, four_down, up, down):
    h = R // 2
    up[:h] = (kept[1, :h] + three_up[:h].astype(F32) + four_up[...].astype(F32)).astype(BF16)
    up[h:] = (kept[1, h:] + three_up[h:].astype(F32)).astype(BF16)
    down[:h] = (kept[2, :h] + three_down[:h].astype(F32)).astype(BF16)
    down[h:] = (kept[2, h:] + three_down[h:].astype(F32) + four_down[...].astype(F32)).astype(BF16)


def between(*parts):
    return pl.pallas_call(
        between_kernel,
        out_shape=[jax.ShapeDtypeStruct((R, F), BF16)] * 2,
        compiler_params=pltpu.CompilerParams(vmem_limit_bytes=16 * MIB),
        cost_estimate=pl.CostEstimate(flops=8 * R * F, bytes_accessed=20 * R * F, transcendentals=0),
    )(*parts)


def swap(v):
    return lax.ppermute(v, "c", [(0, 1), (1, 0)])


def after(v, *others):
    return lax.optimization_barrier((v, *others))[0]


def leg(blocks, axes):
    out = [blocks[0]]
    for k in (2, 1, 3):
        pairs = []
        for x in range(4):
            for y in range(4):
                for c in range(2):
                    to = ((x + k) % 4, y) if axes[c] == "x" else (x, (y + k) % 4)
                    pairs.append(((x * 4 + y) * 2 + c, (to[0] * 4 + to[1]) * 2 + c))
        out.append(lax.ppermute(blocks[k], XYC, pairs))
    return out


def on_device(context, residual, out_proj, norm_gain, cotangent, probe_seed):
    x, zh, y, zl, c = (lax.axis_index(a).astype(INT) for a in AXES)
    info = jnp.concatenate([jnp.stack([x, y, zh * 4 + zl, c]), probe_seed])

    rest, gain = regroup(info, residual, cotangent, norm_gain)
    rows = lax.all_to_all(context.reshape(8, OWN, F), T, 0, 0, tiled=True)
    rows, rest, gain = lax.optimization_barrier((rows, rest, gain))

    came = lax.optimization_barrier(leg(first_leg(rows, rest), "xy"))
    came = [came[n] for n in (0, 2, 1, 3)]
    behind, ahead = shift(out_proj, Z, 1), shift(out_proj, Z, -1)
    two, ahead2 = after(jnp.stack([out_proj, behind]), rows), after(jnp.stack([out_proj, ahead]), rows)
    behind2, ahead2 = shift(two, Z, 2), shift(ahead2, Z, -2)
    far = shift(after(ahead2[1], *came), Z, -1)
    own = jnp.concatenate([two, behind2, far[None], ahead2[::-1], ahead[None]])

    probe = make_probe(after(info, *came))
    *pieces, probe, own = lax.optimization_barrier((*leg(second_leg(info, came), "yx"), probe, own))
    pieces = [pieces[n] for n in (0, 2, 1, 3)]
    other = swap(own)
    rows, res, u, w = tangent_of(info, pieces, probe, gain)
    s, stats = stream_of(info, own, other, rows, res, u, w)
    stats = lax.all_to_all(jnp.broadcast_to(stats[None], (16, 8, TOK)), XY, 0, 0, tiled=True)
    grad, send = away(info, stats, s, u, w, rows)
    near_up, near_down, three_up, three_down, four_up, four_down, kept = home(info, grad, rows, swap(send))

    four_up, four_down, three_up, three_down = lax.optimization_barrier(
        (shift(four_up, Z, 2), shift(four_down, Z, -2), shift(three_up, Z, 1), shift(three_down, Z, -1))
    )
    near_up, near_down = shift(near_up, Z, 1), shift(near_down, Z, -1)
    up, down = between(kept, three_up, three_down, four_up, four_down)
    up, down = shift(up, Z, 2), shift(down, Z, -2)
    return last(info, kept, near_up, near_down, up, down)


def solution(mesh):
    split = Mesh(mesh.devices.reshape(GRID), AXES)
    dp, tensor = ("x", "zh", "y"), T
    in_specs = (
        P(dp, tensor),
        P((*dp, *tensor), None),
        P(dp, tensor),
        P(),
        P((*dp, *tensor), None),
        P(),
    )
    return jax.shard_map(on_device, mesh=split, in_specs=in_specs, out_specs=P(dp, tensor), check_vma=False)
```

```python
import jax
import jax.numpy as jnp
from jax import lax
from jax.experimental import pallas as pl
from jax.experimental.pallas import tpu as pltpu
from jax.sharding import Mesh
from jax.sharding import PartitionSpec as P

AXES = ("x", "zh", "y", "zl", "c")
GRID = (4, 2, 4, 4, 2)
Z = ("zh", "zl")
XY = ("x", "y")
T = ("zl", "c")
R = 192
F = 384
W = 8 * F
OWN = 32
TOK = 16 * OWN
D = 2 * R
N = 32 * R
E = W + 2 * D
XYC = ("x", "y", "c")
MIB = 1024 * 1024
MULT = 747796405
INT = jnp.int32
F32 = jnp.float32
BF16 = jnp.bfloat16
NT = (((1,), (1,)), ((), ()))


def shift(v, axis, k):
    n = 8 if axis == Z else 4
    return lax.ppermute(v, axis, [(s, (s + k) % n) for s in range(n)])


def parity(info, rows, cols):
    m = (rows * W * INT(MULT) + info[4]) + cols * INT(MULT)
    m = m ^ lax.shift_right_logical(m, INT(16))
    m = m * INT(73244475)
    m = m ^ info[5]
    m = m ^ lax.shift_right_logical(m, INT(15))
    return lax.shift_right_logical(m, INT(9)) & INT(1)


def probe_kernel(info, out):
    x, y = info[0], info[1]
    cols = lax.broadcasted_iota(INT, (1, F), 1) + pl.program_id(0) * F
    rows = lax.broadcasted_iota(INT, (R, 1), 0)
    for zh in range(2):
        d = rows + (x * 8 + zh * 4 + y) * R
        out[zh * R : (zh + 1) * R, :] = (1 - 2 * parity(info, d, cols)).astype(F32).astype(BF16)


def make_probe(info):
    return pl.pallas_call(
        probe_kernel,
        grid=(8,),
        in_specs=[pl.BlockSpec(memory_space=pltpu.SMEM)],
        out_specs=pl.BlockSpec((D, F), lambda j: (0, j)),
        out_shape=jax.ShapeDtypeStruct((D, W), BF16),
        compiler_params=pltpu.CompilerParams(vmem_limit_bytes=16 * MIB),
        cost_estimate=pl.CostEstimate(flops=14 * D * W, bytes_accessed=2 * D * W, transcendentals=0),
    )(info)


def regroup_kernel(info, residual, cotangent, gains, out, gain):
    x, y, c = info[0], info[1], info[3]
    eye = lax.broadcasted_iota(INT, (R, R), 0) == lax.broadcasted_iota(INT, (R, R), 1)
    for zh in range(2):
        row = gains[pl.ds(x * 8 + zh * 4 + y, 1), :]
        gain[zh * R : (zh + 1) * R, :] = jnp.sum(jnp.where(eye, row, 0.0), axis=1, keepdims=True)

    @pl.when(c == 0)
    def _():
        for n, v in enumerate((residual, cotangent)):
            for k in range(4):
                part = v[:, pl.ds(pl.multiple_of((x + k) % 4 * (8 * R), 8 * R), 8 * R)]
                for at in range(4):
                    for zh in range(2):
                        first = at * 2 * D + n * D + zh * R
                        out[k, :, first : first + R] = part[:, (zh * 4 + at) * R : (zh * 4 + at + 1) * R]

    @pl.when(c == 1)
    def _():
        for n, v in enumerate((residual, cotangent)):
            for at in range(4):
                part = v[:, at * 8 * R : (at + 1) * 8 * R]
                for to in range(4):
                    k = (to - y + 4) % 4
                    for zh in range(2):
                        first = at * 2 * D + n * D + zh * R
                        out[k, :, first : first + R] = part[:, (zh * 4 + to) * R : (zh * 4 + to + 1) * R]


def regroup(info, residual, cotangent, norm_gain):
    return pl.pallas_call(
        regroup_kernel,
        in_specs=[pl.BlockSpec(memory_space=pltpu.SMEM)] + [pl.BlockSpec(memory_space=pltpu.VMEM)] * 3,
        out_shape=[jax.ShapeDtypeStruct((4, OWN, 8 * D), BF16), jax.ShapeDtypeStruct((D, 1), F32)],
        compiler_params=pltpu.CompilerParams(vmem_limit_bytes=16 * MIB),
        cost_estimate=pl.CostEstimate(flops=0, bytes_accessed=8 * OWN * N, transcendentals=0),
    )(info, residual, cotangent, norm_gain.reshape(32, R))


def first_kernel(rows, rest, *out):
    for k in range(4):
        for t in range(8):
            out[k][:OWN, t * F : (t + 1) * F] = rows[t]
        out[k][OWN:] = rest[k]


def first_leg(rows, rest):
    return pl.pallas_call(
        first_kernel,
        out_shape=[jax.ShapeDtypeStruct((2 * OWN, W), BF16)] * 4,
        compiler_params=pltpu.CompilerParams(vmem_limit_bytes=16 * MIB),
        cost_estimate=pl.CostEstimate(flops=0, bytes_accessed=32 * OWN * W, transcendentals=0),
    )(rows, rest)


def second_kernel(info, *refs):
    came, out = refs[:4], refs[4:]
    place = jnp.where(info[3] == 0, info[1], info[0])
    for j in range(4):
        columns = pl.ds(pl.multiple_of((place + j) % 4 * 2 * D, 2 * D), 2 * D)
        for k in range(4):
            out[j][k, :, :W] = came[k][:OWN]
            out[j][k, :, W:] = came[k][OWN:, columns]


def second_leg(info, came):
    return pl.pallas_call(
        second_kernel,
        in_specs=[pl.BlockSpec(memory_space=pltpu.SMEM)] + [pl.BlockSpec(memory_space=pltpu.VMEM)] * 4,
        out_shape=[jax.ShapeDtypeStruct((4, OWN, E), BF16)] * 4,
        compiler_params=pltpu.CompilerParams(vmem_limit_bytes=16 * MIB),
        cost_estimate=pl.CostEstimate(flops=0, bytes_accessed=64 * OWN * E, transcendentals=0),
    )(info, *came)


def tangent_kernel(info, *refs):
    pieces, (probe, gain), (context, r_out, u_out, w_out), (residual, cotangent) = refs[:4], refs[4:6], refs[6:10], refs[10:]
    x, y, c = info[0], info[1], info[3]
    for j in range(4):
        for k in range(4):
            ax = (x - jnp.where(c == 0, k, j) + 4) % 4
            ay = (y - jnp.where(c == 0, j, k) + 4) % 4
            row = pl.ds(pl.multiple_of((ax * 4 + ay) * OWN, OWN), OWN)
            context[row, :] = pieces[j][k, :, :W]
            residual[row, :] = pieces[j][k, :, W : W + D]
            cotangent[row, :] = pieces[j][k, :, W + D :]
    u_out[...] = lax.dot_general(probe[...], context[...], NT, preferred_element_type=F32)
    w_out[...] = turned(cotangent[...]) * gain[...]
    r_out[...] = turned(residual[...])


def turned(v):
    eye = (lax.broadcasted_iota(INT, (D, D), 0) == lax.broadcasted_iota(INT, (D, D), 1)).astype(F32).astype(BF16)
    return lax.dot_general(eye, v, NT, preferred_element_type=F32)


def tangent_of(info, pieces, probe, gain):
    return pl.pallas_call(
        tangent_kernel,
        in_specs=[pl.BlockSpec(memory_space=pltpu.SMEM)] + [pl.BlockSpec(memory_space=pltpu.VMEM)] * 6,
        out_shape=[jax.ShapeDtypeStruct((TOK, W), BF16)] + [jax.ShapeDtypeStruct((D, TOK), F32)] * 3,
        scratch_shapes=[pltpu.VMEM((TOK, D), BF16)] * 2,
        compiler_params=pltpu.CompilerParams(vmem_limit_bytes=16 * MIB),
        cost_estimate=pl.CostEstimate(flops=2 * D * TOK * W, bytes_accessed=8 * TOK * W, transcendentals=0),
    )(info, *pieces, probe, gain)


def stream_kernel(info, own, other, context, residual, u_in, w_in, s_out, stats, weight):
    zr, c = info[2], info[3]
    for zh in range(2):
        for zl in range(4):
            at = (zr - (zh * 4 + zl) + 8) % 8
            rows = slice(zh * R, (zh + 1) * R)
            weight[rows, pl.ds(pl.multiple_of((zl * 2 + c) * F, F), F)] = own[at]
            weight[rows, pl.ds(pl.multiple_of((zl * 2 + 1 - c) * F, F), F)] = other[at]
    s = residual[...] + lax.dot_general(weight[...], context[...], NT, preferred_element_type=F32)
    s_out[...] = s
    u, w = u_in[...], w_in[...]
    mean = lambda v: jnp.sum(v, axis=0, keepdims=True) * (1.0 / D)
    ms, mu, mw = mean(s), mean(u), mean(w)
    sc, uc, wc = s - ms, u - mu, w - mw
    stats[0:1] = ms
    stats[1:2] = mu
    stats[2:3] = mw
    stats[3:4] = mean(sc * sc)
    stats[4:5] = mean(sc * uc)
    stats[5:6] = mean(sc * wc)
    stats[6:7] = mean(uc * wc)
    stats[7:8] = jnp.zeros_like(ms)


def stream_of(info, own, other, context, residual, u, w):
    return pl.pallas_call(
        stream_kernel,
        in_specs=[pl.BlockSpec(memory_space=pltpu.SMEM)] + [pl.BlockSpec(memory_space=pltpu.VMEM)] * 6,
        out_shape=[jax.ShapeDtypeStruct((D, TOK), F32), jax.ShapeDtypeStruct((8, TOK), F32)],
        scratch_shapes=[pltpu.VMEM((D, W), BF16)],
        compiler_params=pltpu.CompilerParams(vmem_limit_bytes=16 * MIB),
        cost_estimate=pl.CostEstimate(flops=2 * D * TOK * W, bytes_accessed=8 * TOK * W, transcendentals=0),
    )(info, own, other, context, residual, u, w)


def gradient(stats, s, u, w):
    parts = [stats[j] for j in range(16)]
    total = parts[0]
    for part in parts[1:]:
        total = total + part
    mean = total * (1.0 / 16)
    ms, mu, mw = mean[0:1], mean[1:2], mean[2:3]
    css, csu, csw, cuw = mean[3:4], mean[4:5], mean[5:6], mean[6:7]
    for part in parts:
        ds, du, dw = part[0:1] - ms, part[1:2] - mu, part[2:3] - mw
        css = css + ds * ds * (1.0 / 16)
        csu = csu + ds * du * (1.0 / 16)
        csw = csw + ds * dw * (1.0 / 16)
        cuw = cuw + du * dw * (1.0 / 16)
    r2 = 1.0 / (css + 1e-05)
    r = lax.rsqrt(css + 1e-05)
    k = -(r * r2)
    gamma = cuw - 3.0 * r2 * csu * csw
    value = k * (csu * (w[...] - mw) + csw * (u[...] - mu) + gamma * (s[...] - ms))
    return value.astype(BF16)


def owner(info, k):
    chip = (info[2] + k) % 8
    return pl.ds(pl.multiple_of(chip // 4 * R, R), R), chip % 4 * 2


def away_kernel(info, stats, s, u, w, context, grad, send):
    grad[...] = gradient(stats, s, u, w)
    for k in range(8):
        rows, feature = owner(info, k)
        columns = context[:, pl.ds(pl.multiple_of((feature + 1 - info[3]) * F, F), F)]
        send[k] = jnp.dot(grad[rows, :], columns, preferred_element_type=F32).astype(BF16)


def away(info, stats, s, u, w, context):
    return pl.pallas_call(
        away_kernel,
        in_specs=[pl.BlockSpec(memory_space=pltpu.SMEM)] + [pl.BlockSpec(memory_space=pltpu.VMEM)] * 5,
        out_shape=[jax.ShapeDtypeStruct((D, TOK), BF16), jax.ShapeDtypeStruct((8, R, F), BF16)],
        compiler_params=pltpu.CompilerParams(vmem_limit_bytes=16 * MIB),
        cost_estimate=pl.CostEstimate(flops=D * TOK * W, bytes_accessed=8 * TOK * W, transcendentals=0),
    )(info, stats, s, u, w, context)


def home_kernel(info, grad, context, received, near_up, near_down, three_up, three_down, four_up, four_down, kept):
    def part(k):
        rows, feature = owner(info, k)
        columns = context[:, pl.ds(pl.multiple_of((feature + info[3]) * F, F), F)]
        return jnp.dot(grad[rows, :], columns, preferred_element_type=F32) + received[k].astype(F32)

    three_up[...] = part(3).astype(BF16)
    three_down[...] = part(5).astype(BF16)
    four = part(4).astype(BF16)
    four_up[...] = four[: R // 2]
    four_down[...] = four[R // 2 :]
    near_up[...] = part(1).astype(BF16)
    near_down[...] = part(7).astype(BF16)
    for n, k in enumerate((0, 2, 6)):
        kept[n] = part(k)


def home(info, grad, context, received):
    return pl.pallas_call(
        home_kernel,
        in_specs=[pl.BlockSpec(memory_space=pltpu.SMEM)] + [pl.BlockSpec(memory_space=pltpu.VMEM)] * 3,
        out_shape=[jax.ShapeDtypeStruct((R, F), BF16)] * 4
        + [jax.ShapeDtypeStruct((R // 2, F), BF16)] * 2
        + [jax.ShapeDtypeStruct((3, R, F), F32)],
        compiler_params=pltpu.CompilerParams(vmem_limit_bytes=16 * MIB),
        cost_estimate=pl.CostEstimate(flops=D * TOK * W, bytes_accessed=8 * TOK * W, transcendentals=0),
    )(info, grad, context, received)


def last_kernel(info, kept, a, b, up, down, out):
    rows = lax.broadcasted_iota(INT, (R, 1), 0) + (info[0] * 8 + info[2] // 4 * 4 + info[1]) * R
    cols = lax.broadcasted_iota(INT, (1, F), 1) + (info[2] % 4 * 2 + info[3]) * F
    total = kept[0] + a[...].astype(F32) + b[...].astype(F32) + up[...].astype(F32) + down[...].astype(F32)
    out[...] = jnp.where(parity(info, rows, cols) == 0, total, -total)


def last(info, kept, *parts):
    return pl.pallas_call(
        last_kernel,
        in_specs=[pl.BlockSpec(memory_space=pltpu.SMEM)] + [pl.BlockSpec(memory_space=pltpu.VMEM)] * 5,
        out_shape=jax.ShapeDtypeStruct((R, F), F32),
        compiler_params=pltpu.CompilerParams(vmem_limit_bytes=16 * MIB),
        cost_estimate=pl.CostEstimate(flops=20 * R * F, bytes_accessed=20 * R * F, transcendentals=0),
    )(info, kept, *parts)


def between_kernel(kept, three_up, three_down, four_up, four_down, up, down):
    h = R // 2
    up[:h] = (kept[1, :h] + three_up[:h].astype(F32) + four_up[...].astype(F32)).astype(BF16)
    up[h:] = (kept[1, h:] + three_up[h:].astype(F32)).astype(BF16)
    down[:h] = (kept[2, :h] + three_down[:h].astype(F32)).astype(BF16)
    down[h:] = (kept[2, h:] + three_down[h:].astype(F32) + four_down[...].astype(F32)).astype(BF16)


def between(*parts):
    return pl.pallas_call(
        between_kernel,
        out_shape=[jax.ShapeDtypeStruct((R, F), BF16)] * 2,
        compiler_params=pltpu.CompilerParams(vmem_limit_bytes=16 * MIB),
        cost_estimate=pl.CostEstimate(flops=8 * R * F, bytes_accessed=20 * R * F, transcendentals=0),
    )(*parts)


def swap(v):
    return lax.ppermute(v, "c", [(0, 1), (1, 0)])


def after(v, *others):
    return lax.optimization_barrier((v, *others))[0]


def leg(blocks, axes):
    out = [blocks[0]]
    for k in (2, 1, 3):
        pairs = []
        for x in range(4):
            for y in range(4):
                for c in range(2):
                    to = ((x + k) % 4, y) if axes[c] == "x" else (x, (y + k) % 4)
                    pairs.append(((x * 4 + y) * 2 + c, (to[0] * 4 + to[1]) * 2 + c))
        out.append(lax.ppermute(blocks[k], XYC, pairs))
    return out


def on_device(context, residual, out_proj, norm_gain, cotangent, probe_seed):
    x, zh, y, zl, c = (lax.axis_index(a).astype(INT) for a in AXES)
    info = jnp.concatenate([jnp.stack([x, y, zh * 4 + zl, c]), probe_seed])

    rest, gain = regroup(info, residual, cotangent, norm_gain)
    rows = lax.all_to_all(context.reshape(8, OWN, F), T, 0, 0, tiled=True)
    rows, rest, gain = lax.optimization_barrier((rows, rest, gain))

    came = lax.optimization_barrier(leg(first_leg(rows, rest), "xy"))
    came = [came[n] for n in (0, 2, 1, 3)]
    behind, ahead = shift(out_proj, Z, 1), shift(out_proj, Z, -1)
    two, ahead2 = after(jnp.stack([out_proj, behind]), rows), after(jnp.stack([out_proj, ahead]), rows)
    behind2, ahead2 = shift(two, Z, 2), shift(ahead2, Z, -2)
    far = shift(after(ahead2[1], *came), Z, -1)
    own = jnp.concatenate([two, behind2, far[None], ahead2[::-1], ahead[None]])

    probe = make_probe(after(info, *came))
    *pieces, probe, own = lax.optimization_barrier((*leg(second_leg(info, came), "yx"), probe, own))
    pieces = [pieces[n] for n in (0, 2, 1, 3)]
    other = swap(own)
    rows, res, u, w = tangent_of(info, pieces, probe, gain)
    s, stats = stream_of(info, own, other, rows, res, u, w)
    stats = lax.all_to_all(jnp.broadcast_to(stats[None], (16, 8, TOK)), XY, 0, 0, tiled=True)
    grad, send = away(info, stats, s, u, w, rows)
    near_up, near_down, three_up, three_down, four_up, four_down, kept = home(info, grad, rows, swap(send))

    four_up, four_down, three_up, three_down = lax.optimization_barrier(
        (shift(four_up, Z, 2), shift(four_down, Z, -2), shift(three_up, Z, 1), shift(three_down, Z, -1))
    )
    near_up, near_down = shift(near_up, Z, 1), shift(near_down, Z, -1)
    up, down = between(kept, three_up, three_down, four_up, four_down)
    up, down = shift(up, Z, 2), shift(down, Z, -2)
    return last(info, kept, near_up, near_down, up, down)


def solution(mesh):
    split = Mesh(mesh.devices.reshape(GRID), AXES)
    dp, tensor = ("x", "zh", "y"), T
    in_specs = (
        P(dp, tensor),
        P((*dp, *tensor), None),
        P(dp, tensor),
        P(),
        P((*dp, *tensor), None),
        P(),
    )
    return jax.shard_map(on_device, mesh=split, in_specs=in_specs, out_specs=P(dp, tensor), check_vma=False)
```
